512 devices in a mesh: wave: 64 (over x, y, core), fld: 8 (over z).
Axes of the slice: x: 4, y: 8, z: 8, core: 2. Of those that a mesh axis runs over, the one named last changes fastest.
Arguments:
- spec_coeffs: bfloat16 [640, 2, 641, 1024], P('wave', None, None, 'fld'), may hold values from -6 to 6
- legendre: bfloat16 [640, 2, 641, 128], P('wave', None, None, 'fld'), may hold values from -0.15625 to 0.15625
- pair_lower: int32 [640], replicated, may hold values from 0 to 639, each once
- slot_latitude: int32 [256], replicated, may hold values from 0 to 255, each once
- cycle_points: int32 [128], replicated, may hold values from 20 to 5136, as said below
Outputs:
- fourier_bands: bfloat16 [256, 1280, 1024], P('wave', None, 'fld')
The draws below stay inside these ranges and needn't reach their ends.
Inputs may be any that keep to these rules, and one draw needn't show every extreme that they name: Pair slot p holds wavenumbers pair_lower[p] and 1279 - pair_lower[p]; every value appears once. Row s holds northern cycle v for v < 128 and southern cycle v - 128 otherwise, v = slot_latitude[s]; every value appears once. `cycle_points`: each entry is 4 j + 16 for a distinct cycle number j from 1 to 1280; cycles 1 and 1280 are always among them.
All inputs are finite; a program needn't handle non-finite values.
Results may differ from the reference program's by a relative error of at most 0.001.
Values may be sent and summed in bfloat16 or wider, within the bound.
No kernel may reach another device: no remote copies, remote signals or barrier semaphores. Data moves between devices by JAX's collectives and lax.ppermute only.
A program may use at most 64 MiB of HBM per device.

```python
import jax
import jax.numpy as jnp
from jax import lax

TRUNC = 1279
NH = 128
PAIRS = 640
HALF_SLOTS = 641
LATS = 256
COLS = 1024


def draw_cycle_points(key, part):
    key = jax.random.fold_in(key, 7)
    first_key, second_key = jax.random.split(key)
    middle = jax.random.permutation(first_key, TRUNC - 1)[:NH - 2] + 2
    ends = jnp.array([1, TRUNC + 1], dtype=jnp.int32)
    cycles = jnp.concatenate([ends, middle.astype(jnp.int32)])
    cycles = jax.random.permutation(second_key, cycles)
    return (4 * cycles + 16).astype(jnp.int32)


def levels(own_key, dims, cuts, least, top_value):
    gain, own = 1.0, jax.random.fold_in(own_key, 6)
    for dim, blocks in cuts:
        draws = jnp.exp(jax.random.uniform(jax.random.fold_in(own, dim), (blocks,), jnp.float32, least / len(cuts), top_value / len(cuts)))
        gain = gain * jnp.repeat(draws, dims[dim] // blocks).reshape([-1 if axis == dim else 1 for axis in range(len(dims))])
    return gain


def normal_values(key, dims, scale, most, shards=(), held_as=jnp.bfloat16):
    level = levels(key, dims, shards, -0.22, 0.18) if shards else 1.0
    values = jax.random.normal(key, dims, jnp.float32) * scale * level
    return jnp.minimum(jnp.maximum(values, -most), most).astype(held_as)


def setup_inputs(seed: int = 0) -> dict:
    streams_of = jax.random.split(jax.random.key(seed), 6)
    return {
        "spec_coeffs": normal_values(streams_of[0], (PAIRS, 2, HALF_SLOTS, COLS), 1.0, 6.0, ((0, 64), (3, 8))),
        "legendre": normal_values(streams_of[1], (PAIRS, 2, HALF_SLOTS, NH), (TRUNC + 3) ** -0.5, 0.15625, ((0, 64), (3, 8))),
        "pair_lower": jax.random.permutation(streams_of[2], PAIRS).astype(jnp.int32),
        "slot_latitude": jax.random.permutation(streams_of[3], LATS).astype(jnp.int32),
        "cycle_points": draw_cycle_points(jax.random.fold_in(streams_of[5], 71), 0),
    }


def owner_masks(lower_wave, truncation, half_slots):
    slot_index = 2 * lax.broadcasted_iota(jnp.int32, (2, half_slots), 1) + lax.broadcasted_iota(jnp.int32, (2, half_slots), 0)
    slot_index = slot_index[None]
    length = (truncation + 1 - lower_wave).astype(jnp.int32)
    begin = length + length % 2
    lower_b = lower_wave[:, None, None]
    length_b = length[:, None, None]
    begin_b = begin[:, None, None]
    in_lower = slot_index < length_b
    in_upper = (slot_index >= begin_b) & (slot_index <= begin_b + lower_b)
    return jnp.stack([in_lower, in_upper], axis=3).astype(jnp.bfloat16)


def reference(spec_coeffs, legendre, pair_lower, slot_latitude, cycle_points):
    masks = owner_masks(pair_lower, TRUNC, HALF_SLOTS)
    cycle_index = (slot_latitude % NH).astype(jnp.int32)
    cycle_limit = jnp.take(cycle_points, cycle_index)

    def one_pair(pair_items):
        coeffs, pair_table, pair_mask, lower_wave = pair_items
        masked = coeffs.astype(jnp.float32)[:, :, None, :] * pair_mask.astype(jnp.float32)[..., None]
        parity_sums = jnp.einsum("skl,skhc->shlc", pair_table.astype(jnp.float32), masked, precision=lax.Precision.HIGHEST)
        north_part = parity_sums[0] + parity_sums[1]
        south_part = parity_sums[0] - parity_sums[1]
        fourier = jnp.concatenate([north_part, south_part], axis=1).astype(jnp.bfloat16)
        picked = jnp.take(fourier, slot_latitude.astype(jnp.int32), axis=1)
        pair_waves = jnp.stack([lower_wave, TRUNC - lower_wave])
        kept_mask = (2 * pair_waves[:, None] < cycle_limit[None, :]).astype(jnp.bfloat16)
        return picked * kept_mask[..., None]

    result = lax.map(one_pair, (spec_coeffs, legendre, masks, pair_lower))
    result = result.reshape(2 * PAIRS, LATS, COLS)
    pair_index = jnp.arange(PAIRS, dtype=jnp.int32)
    wave_of = jnp.zeros((TRUNC + 1,), jnp.int32).at[pair_lower].set(2 * pair_index)
    wave_of = wave_of.at[(TRUNC - pair_lower).astype(jnp.int32)].set(2 * pair_index + 1)
    return jnp.transpose(jnp.take(result, wave_of, axis=0), (1, 0, 2))
```

```python
import functools

import jax
import jax.numpy as jnp
from jax import lax
from jax.experimental import pallas as pl
from jax.experimental.pallas import tpu as pltpu
from jax.sharding import PartitionSpec as P

BF = jnp.bfloat16
F32 = jnp.float32
LANES = 128
ROWS = 16
VMEM_LIMIT = 48 * 1024 * 1024


def whole(shape):
    return pl.BlockSpec(shape, lambda *_: (0,) * len(shape))


def pack_kernel(table_ref, *out_refs):
    pairs, _, rows, half_slots = table_ref.shape
    blocks = half_slots // LANES
    group = pairs // len(out_refs)
    lane = lax.broadcasted_iota(jnp.int32, (rows, LANES), 1)
    for g, out_ref in enumerate(out_refs):
        last = jnp.zeros((rows, LANES), F32)
        for i in range(group):
            for r in range(2):
                for b in range(blocks):
                    out_ref[(2 * i + r) * blocks + b] = table_ref[g * group + i, r, :, b * LANES:(b + 1) * LANES]
                tail = table_ref[g * group + i, r, :, half_slots - 1:half_slots].astype(F32)
                last = jnp.where(lane == 2 * i + r, tail, last)
        out_ref[2 * group * blocks] = last.astype(BF)


def pack_table(table, groups):
    pairs, _, rows, half_slots = table.shape
    assert half_slots % LANES == 1
    length = 2 * (pairs // groups) * (half_slots // LANES) + 1
    out = jax.ShapeDtypeStruct((length, rows, LANES), BF)
    return pl.pallas_call(
        pack_kernel,
        out_shape=[out] * groups,
        compiler_params=pltpu.CompilerParams(vmem_limit_bytes=VMEM_LIMIT),
        name="pack_table",
    )(table)


def mask_kernel(truncation, group, place_ref, lower_ref, spec_ref, out_ref):
    _, _, half_slots, columns = spec_ref.shape
    full = half_slots - 1
    i = pl.program_id(0)
    q = lower_ref[place_ref[0] * pl.num_programs(0) + i]
    length = truncation + 1 - q
    begin = length + lax.rem(length, 2)
    for r in range(2):
        slot = 2 * lax.broadcasted_iota(jnp.int32, (full, columns), 0) + r
        coeffs = spec_ref[0, r, :full, :].astype(F32)
        out_ref[0, r, :full, :columns] = jnp.where(slot < length, coeffs, 0.0).astype(BF)
        out_ref[0, r, :full, columns:] = jnp.where((slot >= begin) & (slot <= begin + q), coeffs, 0.0).astype(BF)
        row = lax.broadcasted_iota(jnp.int32, (LANES, columns), 0)
        mine = row == 2 * lax.rem(i, group) + r
        last = 2 * full + r
        tail = spec_ref[0, r, full:, :].astype(F32)
        out_ref[0, r, full:, :columns] = jnp.where(mine & (last < length), tail, 0.0).astype(BF)
        out_ref[0, r, full:, columns:] = jnp.where(mine & (last >= begin) & (last <= begin + q), tail, 0.0).astype(BF)


def mask_coeffs(place, pair_lower, spec, group):
    pairs, _, half_slots, columns = spec.shape
    depth = half_slots - 1 + LANES
    smem = pl.BlockSpec(memory_space=pltpu.SMEM)
    return pl.pallas_call(
        functools.partial(mask_kernel, 2 * half_slots - 3, group),
        grid=(pairs,),
        in_specs=[smem, smem, pl.BlockSpec((1, 2, half_slots, columns), lambda i: (i, 0, 0, 0))],
        out_specs=pl.BlockSpec((1, 2, depth, 2 * columns), lambda i: (i, 0, 0, 0)),
        out_shape=jax.ShapeDtypeStruct((pairs, 2, depth, 2 * columns), BF),
        compiler_params=pltpu.CompilerParams(vmem_limit_bytes=VMEM_LIMIT),
        name="mask_coeffs",
    )(place, pair_lower, spec)


def sums_kernel(truncation, n_wave, groups, place_ref, lower_ref, slots_ref, points_ref, *refs):
    coeff_refs = refs[:groups]
    shard_refs = [refs[groups + 8 * g:groups + 8 * g + 8] for g in range(groups)]
    out_ref, rows_ref, pick_ref, limit_ref = refs[groups + 8 * groups:]
    i = pl.program_id(0)
    steps = pl.num_programs(0)
    pairs = steps * groups
    lats, half = pick_ref.shape[0], pick_ref.shape[0] // 2
    lat_dev = lats // n_wave
    per_dev = out_ref.shape[0] // n_wave
    columns = out_ref.shape[1]
    blocks = coeff_refs[0].shape[2] // LANES - 1

    @pl.when(i == 0)
    def _():
        slots = slots_ref[...]
        cycle = lax.rem(slots, half)
        held = lax.rem(cycle - place_ref[1] * ROWS + half, half) + (slots // half) * half
        index = lax.broadcasted_iota(jnp.int32, (lats, lats), 0)
        pick_ref[...] = jnp.where(index == held, 1.0, 0.0).T.astype(BF)
        index = lax.broadcasted_iota(jnp.int32, (half, lats), 0)
        points = jnp.where(index == cycle, 1.0, 0.0).T * points_ref[...].astype(F32)
        limit_ref[...] = jnp.broadcast_to(jnp.sum(points, axis=1, keepdims=True), limit_ref.shape)

    for g in range(groups):
        pair = i + g * steps
        sums = []
        for r in range(2):
            def block(b):
                return jnp.concatenate([ref[b] for ref in shard_refs[g]], axis=0)

            table = [block((2 * i + r) * blocks + b) for b in range(blocks)] + [block(2 * steps * blocks)]
            sums.append(jnp.dot(jnp.concatenate(table, axis=1), coeff_refs[g][0, r], preferred_element_type=F32))
        both = jnp.concatenate([sums[0] + sums[1], sums[0] - sums[1]], axis=0).astype(BF)
        picked = jnp.dot(pick_ref[...], both, preferred_element_type=F32)
        q = lower_ref[place_ref[0] * pairs + pair]
        for h in range(2):
            wave = (q if h == 0 else truncation - q).astype(F32)
            kept = jnp.where(2.0 * wave < limit_ref[...], picked[:, h * columns:(h + 1) * columns], 0.0)
            for lat in range(lat_dev):
                start = (2 * pair + h) * lat_dev + lat
                rows_ref[pl.ds(start, n_wave, stride=per_dev), :] = kept[lat * n_wave:(lat + 1) * n_wave]

    @pl.when(i == steps - 1)
    def _():
        def body(d, carry):
            at = pl.ds(pl.multiple_of(d * per_dev, per_dev), per_dev)
            out_ref[at, :] = rows_ref[at, :].astype(BF)
            return carry

        lax.fori_loop(0, n_wave, body, 0, unroll=8)


def legendre_sums(place, pair_lower, slots, points, coeffs, shards, n_wave, truncation):
    pairs, _, depth, wide = coeffs.shape
    groups = len(shards)
    steps = pairs // groups
    columns = wide // 2
    lats = slots.shape[1]
    per_dev = 2 * pairs * (lats // n_wave)
    smem = pl.BlockSpec(memory_space=pltpu.SMEM)
    flat = [x for group in shards for x in group]
    return pl.pallas_call(
        functools.partial(sums_kernel, truncation, n_wave, groups),
        grid=(steps,),
        in_specs=[smem, smem, whole(slots.shape), whole(points.shape)]
        + [pl.BlockSpec((1, 2, depth, wide), lambda i, g=g: (i + g * steps, 0, 0, 0)) for g in range(groups)]
        + [whole(x.shape) for x in flat],
        out_specs=whole((n_wave * per_dev, columns)),
        out_shape=jax.ShapeDtypeStruct((n_wave * per_dev, columns), BF),
        scratch_shapes=[
            pltpu.VMEM((n_wave * per_dev, columns), F32),
            pltpu.VMEM((lats, lats), BF),
            pltpu.VMEM((lats, columns), F32),
        ],
        compiler_params=pltpu.CompilerParams(vmem_limit_bytes=VMEM_LIMIT),
        name="legendre_sums",
    )(place, pair_lower, slots, points, *([coeffs] * groups), *flat)


def place_kernel(lat_dev, waves_ref, received_ref, out_ref, rows_ref, held_ref):
    count = waves_ref.shape[1]
    columns = received_ref.shape[1]
    step = received_ref.shape[0] // 64

    def widen(d, carry):
        at = pl.ds(pl.multiple_of(d * step, step), step)
        rows_ref[at, :] = received_ref[at, :].astype(F32)
        return carry

    lax.fori_loop(0, 64, widen, 0, unroll=8)
    for lat in range(lat_dev):
        held_ref[:, lat * columns:(lat + 1) * columns] = rows_ref[pl.ds(lat, count, stride=lat_dev), :].astype(BF)
    tall = 256
    for m in range(0, count, tall):
        index = lax.broadcasted_iota(jnp.int32, (tall, count), 0) + m
        chosen = jnp.where(index == waves_ref[...], 1.0, 0.0).astype(BF)
        placed = jnp.dot(chosen, held_ref[...], preferred_element_type=F32).astype(BF)
        for lat in range(lat_dev):
            out_ref[lat, m:m + tall, :] = placed[:, lat * columns:(lat + 1) * columns]


def place_waves(waves, received, lat_dev):
    count = waves.shape[1]
    columns = received.shape[1]
    return pl.pallas_call(
        functools.partial(place_kernel, lat_dev),
        out_shape=jax.ShapeDtypeStruct((lat_dev, count, columns), BF),
        scratch_shapes=[
            pltpu.VMEM((lat_dev * count, columns), F32),
            pltpu.VMEM((count, lat_dev * columns), BF),
        ],
        compiler_params=pltpu.CompilerParams(vmem_limit_bytes=VMEM_LIMIT),
        name="place_waves",
    )(waves, received)


def gather_ring(groups):
    n = lax.axis_size("fld")
    assert n == 8 and len(groups) == 2

    def up(x):
        return lax.ppermute(x, "fld", [(i, (i + 1) % n) for i in range(n)])

    def down(x):
        return lax.ppermute(x, "fld", [(i, (i - 1) % n) for i in range(n)])

    below, above = [[x] for x in groups], [[x] for x in groups]
    for step in range(n // 2):
        for g in range(2):
            if step < n // 2 - 1 or g == 0:
                below[g].append(up(below[g][-1]))
            if step < n // 2 - 1 or g == 1:
                above[g].append(down(above[g][-1]))
    return [[groups[g]] + above[g][1:] + below[g][:0:-1] for g in range(2)]


def on_device(spec_coeffs, legendre, pair_lower, slot_latitude, cycle_points):
    half_slots = spec_coeffs.shape[2]
    columns = spec_coeffs.shape[3]
    truncation = 2 * half_slots - 3
    n_wave = lax.axis_size("wave")
    lats = slot_latitude.shape[0]
    lat_dev = lats // n_wave
    groups = 2
    place = jnp.stack([lax.axis_index("wave"), lax.axis_index("fld")]).astype(jnp.int32)
    packed = pack_table(jnp.transpose(legendre, (0, 1, 3, 2)), groups)
    shards = gather_ring(packed)
    coeffs = mask_coeffs(place, pair_lower, spec_coeffs, spec_coeffs.shape[0] // groups)
    slots = slot_latitude.reshape(n_wave, lat_dev).T.reshape(1, lats)
    points = cycle_points.reshape(1, lats // 2)
    to_send = legendre_sums(place, pair_lower, slots, points, coeffs, shards, n_wave, truncation)
    to_send = to_send.reshape(n_wave, -1, columns)
    received = lax.all_to_all(to_send, "wave", split_axis=0, concat_axis=0, tiled=True)
    waves = jnp.stack([pair_lower, truncation - pair_lower], axis=1).reshape(1, truncation + 1)
    return place_waves(waves, received.reshape(-1, columns), lat_dev)


def solution(mesh):
    placed = (P("wave", None, None, "fld"), P("wave", None, None, "fld"), P(), P(), P())
    return jax.shard_map(
        on_device, mesh=mesh, in_specs=placed, out_specs=P("wave", None, "fld"), check_vma=False
    )
```

```python
import functools

import jax
import jax.numpy as jnp
from jax import lax
from jax.experimental import pallas as pl
from jax.experimental.pallas import tpu as pltpu
from jax.sharding import PartitionSpec as P

BF = jnp.bfloat16
F32 = jnp.float32
LANES = 128
ROWS = 16
PLAIN = 2
VMEM = pl.BlockSpec(memory_space=pltpu.VMEM)
SMEM = pl.BlockSpec(memory_space=pltpu.SMEM)
PARAMS = pltpu.CompilerParams(vmem_limit_bytes=24 * 1024 * 1024)


def pack_kernel(table_ref, out_ref):
    pairs, _, rows, half_slots = table_ref.shape
    blocks = half_slots // LANES
    lane = lax.broadcasted_iota(jnp.int32, (rows, LANES), 1)
    last = jnp.zeros((rows, LANES), F32)
    for i in range(pairs):
        for r in range(2):
            for b in range(blocks):
                out_ref[(2 * i + r) * blocks + b] = table_ref[i, r, :, b * LANES:(b + 1) * LANES]
            tail = table_ref[i, r, :, half_slots - 1:half_slots].astype(F32)
            last = jnp.where(lane == 2 * i + r, tail, last)
    out_ref[2 * pairs * blocks] = last.astype(BF)


def pack_table(table):
    pairs, _, rows, half_slots = table.shape
    assert half_slots % LANES == 1
    return pl.pallas_call(
        pack_kernel,
        in_specs=[VMEM],
        out_specs=VMEM,
        out_shape=jax.ShapeDtypeStruct((2 * pairs * (half_slots // LANES) + 1, rows, LANES), BF),
        compiler_params=PARAMS,
        name="pack_table",
    )(table)


def rows_kernel(place_ref, slots_ref, points_ref, pick_ref, limit_ref):
    slots = slots_ref[...]
    lats = slots.shape[1]
    half = lats // 2
    cycle = lax.rem(slots, half)
    held = lax.rem(cycle - place_ref[1] * ROWS + half, half) + (slots // half) * half
    index = lax.broadcasted_iota(jnp.int32, (lats, lats), 0)
    pick_ref[...] = jnp.where(index == held, 1.0, 0.0).T.astype(BF)
    index = lax.broadcasted_iota(jnp.int32, (half, lats), 0)
    points = jnp.where(index == cycle, 1.0, 0.0).T * points_ref[...].astype(F32)
    limit_ref[...] = jnp.broadcast_to(jnp.sum(points, axis=1, keepdims=True), limit_ref.shape)


def row_order(place, slots, points):
    lats = slots.shape[1]
    return pl.pallas_call(
        rows_kernel,
        in_specs=[SMEM, VMEM, VMEM],
        out_specs=[VMEM, VMEM],
        out_shape=[jax.ShapeDtypeStruct((lats, lats), BF), jax.ShapeDtypeStruct((lats, LANES), F32)],
        compiler_params=PARAMS,
        name="row_order",
    )(place, slots, points)


def sums_kernel(truncation, n_wave, place_ref, lower_ref, pick_ref, limit_ref, spec_ref, *refs):
    shard_refs, out_ref, rows_ref = refs[:9], refs[9], refs[10]
    pairs, _, half_slots, columns = spec_ref.shape
    lat_dev = pick_ref.shape[0] // n_wave
    per_dev = out_ref.shape[0] // n_wave
    full = half_slots - 1
    blocks = full // LANES
    plain = PLAIN * LANES
    group = pairs // 2
    split = 2 * group * blocks

    def block(b, g):
        low, high = shard_refs[4], shard_refs[5]
        parts = [ref[g * split + b] for ref in shard_refs[:4]]
        parts.append(low[b] if g == 0 else high[b])
        parts += [ref[g * split + b] for ref in shard_refs[6:]]
        return jnp.concatenate(parts, axis=0)

    tails = block(split, 1)

    def step(i, carry):
        for g in range(2):
            pair = i + g * group
            q = lower_ref[place_ref[0] * pairs + pair]
            length = truncation + 1 - q
            begin = length + lax.rem(length, 2)
            sums = []
            for r in range(2):
                def owned(slot, coeffs, lower):
                    kept = slot < length if lower else (slot >= begin) & (slot <= begin + q)
                    return jnp.where(kept, coeffs, 0.0).astype(BF)

                first = 2 * i * blocks + r * blocks
                table = [block(first + b, g) for b in range(blocks)]
                below = jnp.dot(
                    jnp.concatenate(table[:PLAIN], axis=1), spec_ref[pair, r, :plain, :], preferred_element_type=F32
                )
                coeffs = spec_ref[pair, r, plain:full, :].astype(F32)
                slot = 2 * (lax.broadcasted_iota(jnp.int32, coeffs.shape, 0) + plain) + r
                row = lax.broadcasted_iota(jnp.int32, (LANES, columns), 0)
                tail = jnp.where(row == 2 * pair + r, spec_ref[pair, r, full:, :].astype(F32), 0.0)
                last = jnp.full((LANES, columns), 2 * full + r, jnp.int32)
                both = [
                    jnp.concatenate([owned(slot, coeffs, lower), owned(last, tail, lower)], axis=0)
                    for lower in (True, False)
                ]
                above = jnp.dot(
                    jnp.concatenate(table[PLAIN:] + [tails], axis=1),
                    jnp.concatenate(both, axis=1),
                    preferred_element_type=F32,
                )
                sums.append((above[:, :columns] + below, above[:, columns:]))
            north = jnp.concatenate([sums[0][h] + sums[1][h] for h in range(2)], axis=1)
            south = jnp.concatenate([sums[0][h] - sums[1][h] for h in range(2)], axis=1)
            fourier = jnp.concatenate([north, south], axis=0).astype(BF)
            picked = jnp.dot(pick_ref[...], fourier, preferred_element_type=F32)
            for h in range(2):
                wave = (q if h == 0 else truncation - q).astype(F32)
                kept = jnp.where(2.0 * wave < limit_ref[...], picked[:, h * columns:(h + 1) * columns], 0.0)
                for lat in range(lat_dev):
                    start = (2 * pair + h) * lat_dev + lat
                    rows_ref[pl.ds(start, n_wave, stride=per_dev), :] = kept[lat * n_wave:(lat + 1) * n_wave]
        return carry

    lax.fori_loop(0, group, step, 0)

    def narrow(d, carry):
        at = pl.ds(pl.multiple_of(d * per_dev, per_dev), per_dev)
        out_ref[at, :] = rows_ref[at, :].astype(BF)
        return carry

    lax.fori_loop(0, n_wave, narrow, 0, unroll=8)


def legendre_sums(place, pair_lower, pick, limit, spec, shards, n_wave, truncation):
    pairs, _, _, columns = spec.shape
    sent = 2 * pairs * pick.shape[0]
    return pl.pallas_call(
        functools.partial(sums_kernel, truncation, n_wave),
        in_specs=[SMEM, SMEM] + [VMEM] * (3 + len(shards)),
        out_specs=VMEM,
        out_shape=jax.ShapeDtypeStruct((sent, columns), BF),
        scratch_shapes=[pltpu.VMEM((sent, columns), F32)],
        compiler_params=PARAMS,
        name="legendre_sums",
    )(place, pair_lower, pick, limit, spec, *shards)


def order_kernel(waves_ref, out_ref):
    count, tall = waves_ref.shape[1], 256
    for m in range(0, count, tall):
        index = lax.broadcasted_iota(jnp.int32, (tall, count), 0) + m
        out_ref[m:m + tall, :] = jnp.where(index == waves_ref[...], 1.0, 0.0).astype(BF)


def wave_order(waves):
    count = waves.shape[1]
    return pl.pallas_call(
        order_kernel,
        in_specs=[VMEM],
        out_specs=VMEM,
        out_shape=jax.ShapeDtypeStruct((count, count), BF),
        compiler_params=PARAMS,
        name="wave_order",
    )(waves)


def place_kernel(chosen_ref, received_ref, out_ref, rows_ref, held_ref):
    lat_dev, count, columns = out_ref.shape
    pieces = 64
    step = received_ref.shape[0] // pieces

    def widen(d, carry):
        at = pl.ds(pl.multiple_of(d * step, step), step)
        rows_ref[at, :] = received_ref[at, :].astype(F32)
        return carry

    lax.fori_loop(0, pieces, widen, 0, unroll=8)
    for lat in range(lat_dev):
        held_ref[:, lat * columns:(lat + 1) * columns] = rows_ref[pl.ds(lat, count, stride=lat_dev), :].astype(BF)
    tall = 256
    for m in range(0, count, tall):
        placed = jnp.dot(chosen_ref[m:m + tall, :], held_ref[...], preferred_element_type=F32).astype(BF)
        for lat in range(lat_dev):
            out_ref[lat, m:m + tall, :] = placed[:, lat * columns:(lat + 1) * columns]


def place_waves(chosen, received, lat_dev):
    count = chosen.shape[0]
    columns = received.shape[1]
    return pl.pallas_call(
        place_kernel,
        in_specs=[VMEM, VMEM],
        out_specs=VMEM,
        out_shape=jax.ShapeDtypeStruct((lat_dev, count, columns), BF),
        scratch_shapes=[
            pltpu.VMEM((lat_dev * count, columns), F32),
            pltpu.VMEM((count, lat_dev * columns), BF),
        ],
        compiler_params=PARAMS,
        name="place_waves",
    )(chosen, received)


def on_device(spec_coeffs, legendre, pair_lower, slot_latitude, cycle_points):
    pairs, _, half_slots, columns = spec_coeffs.shape
    truncation = 2 * half_slots - 3
    n_wave, n_fld = lax.axis_size("wave"), lax.axis_size("fld")
    lats = slot_latitude.shape[0]
    lat_dev = lats // n_wave
    assert n_fld == 8

    def up(x):
        return lax.ppermute(x, "fld", [(i, (i + 1) % n_fld) for i in range(n_fld)])

    def down(x):
        return lax.ppermute(x, "fld", [(i, (i - 1) % n_fld) for i in range(n_fld)])

    place = jnp.stack([lax.axis_index("wave"), lax.axis_index("fld")]).astype(jnp.int32)
    slots = slot_latitude.reshape(n_wave, lat_dev).T.reshape(1, lats)
    points = cycle_points.reshape(1, lats // 2)
    waves = jnp.stack([pair_lower, truncation - pair_lower], axis=1).reshape(1, truncation + 1)

    own = pack_table(jnp.transpose(legendre, (0, 1, 3, 2)))
    half = (own.shape[0] - 1) // 2
    below1, above1 = up(own), down(own)
    below1, spec = lax.optimization_barrier((below1, spec_coeffs))
    below2, above2 = up(below1), down(above1)
    pick, limit = row_order(place, slots, points)
    below2, pick, limit, waves = lax.optimization_barrier((below2, pick, limit, waves))
    below3, above3 = up(below2), down(above2)
    low, high = up(below3[:half]), down(above3[half:])
    shards = [own, above1, above2, above3, low, high, below3, below2, below1]
    to_send = legendre_sums(place, pair_lower, pick, limit, spec, shards, n_wave, truncation)
    to_send, waves = lax.optimization_barrier((to_send, waves))
    received = lax.all_to_all(to_send.reshape(n_wave, -1, columns), "wave", split_axis=0, concat_axis=0, tiled=True)
    return place_waves(wave_order(waves), received.reshape(-1, columns), lat_dev)


def solution(mesh):
    placed = (P("wave", None, None, "fld"), P("wave", None, None, "fld"), P(), P(), P())
    return jax.shard_map(
        on_device, mesh=mesh, in_specs=placed, out_specs=P("wave", None, "fld"), check_vma=False
    )
```

```python
import functools

import jax
import jax.numpy as jnp
from jax import lax
from jax.experimental import pallas as pl
from jax.experimental.pallas import tpu as pltpu
from jax.sharding import PartitionSpec as P

BF = jnp.bfloat16
F32 = jnp.float32
LANES = 128
ROWS = 16
PLAIN = 2
VMEM = pl.BlockSpec(memory_space=pltpu.VMEM)
SMEM = pl.BlockSpec(memory_space=pltpu.SMEM)
PIECE = 80
UNROLL = True
PARAMS = pltpu.CompilerParams(vmem_limit_bytes=24 * 1024 * 1024)


def pack_kernel(table_ref, *out_refs):
    pairs, _, rows, half_slots = table_ref.shape
    blocks = half_slots // LANES
    group = pairs // len(out_refs)
    lane = lax.broadcasted_iota(jnp.int32, (rows, LANES), 1)
    for g, out_ref in enumerate(out_refs):
        last = jnp.zeros((rows, LANES), F32)
        for i in range(group):
            for r in range(2):
                for b in range(blocks):
                    out_ref[(2 * i + r) * blocks + b] = table_ref[g * group + i, r, :, b * LANES:(b + 1) * LANES]
                tail = table_ref[g * group + i, r, :, half_slots - 1:half_slots].astype(F32)
                last = jnp.where(lane == 2 * i + r, tail, last)
        out_ref[2 * group * blocks] = last.astype(BF)


def pack_table(table, groups):
    pairs, _, rows, half_slots = table.shape
    assert half_slots % LANES == 1
    length = 2 * (pairs // groups) * (half_slots // LANES) + 1
    return pl.pallas_call(
        pack_kernel,
        in_specs=[VMEM],
        out_specs=[VMEM] * groups,
        out_shape=[jax.ShapeDtypeStruct((length, rows, LANES), BF)] * groups,
        compiler_params=PARAMS,
        name="pack_table",
    )(table)


def rows_kernel(lat_dev, place_ref, slots_ref, points_ref, pick_ref, limit_ref):
    lats = slots_ref.shape[1]
    half = lats // 2
    n_wave = lats // lat_dev
    sent = lax.broadcasted_iota(jnp.int32, (lats, lats), 1)
    source = lax.rem(sent, n_wave) * lat_dev + sent // n_wave
    moved = jnp.where(lax.broadcasted_iota(jnp.int32, (lats, lats), 0) == source, 1.0, 0.0).astype(BF)
    slots = jnp.broadcast_to(slots_ref[...].astype(F32), (ROWS, lats)).astype(BF)
    slots = jnp.dot(slots, moved, preferred_element_type=F32)[:1].astype(jnp.int32)
    cycle = lax.rem(slots, half)
    held = lax.rem(cycle - place_ref[1] * ROWS + half, half) + (slots // half) * half
    index = lax.broadcasted_iota(jnp.int32, (lats, lats), 0)
    pick_ref[...] = jnp.where(index == held, 1.0, 0.0).T.astype(BF)
    index = lax.broadcasted_iota(jnp.int32, (half, lats), 0)
    points = jnp.where(index == cycle, 1.0, 0.0).T * points_ref[...].astype(F32)
    limit_ref[...] = jnp.broadcast_to(jnp.sum(points, axis=1, keepdims=True), limit_ref.shape)


def row_order(place, slots, points, lat_dev):
    lats = slots.shape[1]
    assert lats <= 256
    return pl.pallas_call(
        functools.partial(rows_kernel, lat_dev),
        in_specs=[SMEM, VMEM, VMEM],
        out_specs=[VMEM, VMEM],
        out_shape=[jax.ShapeDtypeStruct((lats, lats), BF), jax.ShapeDtypeStruct((lats, LANES), F32)],
        compiler_params=PARAMS,
        name="row_order",
    )(place, slots, points)


def sums_kernel(truncation, n_wave, first_pair, last_group, place_ref, lower_ref, pick_ref, limit_ref, spec_ref, *refs):
    shard_refs, earlier, out_ref = refs[:8], refs[8:-2] if last_group else (), refs[-2] if last_group else refs[-1]
    rows_ref = refs[-1]
    all_pairs, _, half_slots, columns = spec_ref.shape
    lat_dev = pick_ref.shape[0] // n_wave
    per_dev = rows_ref.shape[0] // n_wave
    group = per_dev // (2 * lat_dev)
    full = half_slots - 1
    blocks = full // LANES
    plain = PLAIN * LANES

    def block(b, g):
        return jnp.concatenate([ref[b] for ref in shard_refs], axis=0)

    def step(i, carry):
        for g in range(1):
            local = i
            pair = local + first_pair
            q = lower_ref[place_ref[0] * all_pairs + pair]
            length = truncation + 1 - q
            begin = length + lax.rem(length, 2)
            tails = block(2 * group * blocks, g)
            sums = []
            for r in range(2):
                def owned(slot, coeffs, lower):
                    kept = slot < length if lower else (slot >= begin) & (slot <= begin + q)
                    return jnp.where(kept, coeffs, 0.0).astype(BF)

                table = [block((2 * i + r) * blocks + b, g) for b in range(blocks)]
                below = jnp.dot(
                    jnp.concatenate(table[:PLAIN], axis=1), spec_ref[pair, r, :plain, :], preferred_element_type=F32
                )
                coeffs = spec_ref[pair, r, plain:full, :].astype(F32)
                slot = 2 * (lax.broadcasted_iota(jnp.int32, coeffs.shape, 0) + plain) + r
                row = lax.broadcasted_iota(jnp.int32, (LANES, columns), 0)
                tail = jnp.where(row == 2 * i + r, spec_ref[pair, r, full:, :].astype(F32), 0.0)
                last = jnp.full((LANES, columns), 2 * full + r, jnp.int32)
                both = [
                    jnp.concatenate([owned(slot, coeffs, lower), owned(last, tail, lower)], axis=0)
                    for lower in (True, False)
                ]
                above = jnp.dot(
                    jnp.concatenate(table[PLAIN:] + [tails], axis=1),
                    jnp.concatenate(both, axis=1),
                    preferred_element_type=F32,
                )
                sums.append((above[:, :columns] + below, above[:, columns:]))
            north = jnp.concatenate([sums[0][h] + sums[1][h] for h in range(2)], axis=1)
            south = jnp.concatenate([sums[0][h] - sums[1][h] for h in range(2)], axis=1)
            fourier = jnp.concatenate([north, south], axis=0).astype(BF)
            picked = jnp.dot(pick_ref[...], fourier, preferred_element_type=F32)
            for h in range(2):
                wave = (q if h == 0 else truncation - q).astype(F32)
                kept = jnp.where(2.0 * wave < limit_ref[...], picked[:, h * columns:(h + 1) * columns], 0.0)
                for lat in range(lat_dev):
                    start = (2 * local + h) * lat_dev + lat
                    rows_ref[pl.ds(start, n_wave, stride=per_dev), :] = kept[lat * n_wave:(lat + 1) * n_wave]
        return carry

    lax.fori_loop(0, group, step, 0, unroll=UNROLL)

    def narrow(d, carry):
        at = pl.ds(pl.multiple_of(d * per_dev, per_dev), per_dev)
        parts = [ref[at, :] for ref in earlier + (rows_ref,)]
        sent = per_dev * len(parts)
        out_ref[pl.ds(pl.multiple_of(d * sent, sent), sent), :] = jnp.concatenate(parts, axis=0).astype(BF)
        return carry

    if last_group:
        lax.fori_loop(0, n_wave, narrow, 0, unroll=8)


def legendre_sums(place, pair_lower, pick, limit, spec, shards, earlier, first_pair, group, last, n_wave, truncation):
    columns = spec.shape[3]
    rows = 2 * group * pick.shape[0]
    if last:
        out = jax.ShapeDtypeStruct((rows * (1 + len(earlier)), columns), BF)
    else:
        out, earlier = jax.ShapeDtypeStruct((rows, columns), F32), []
    return pl.pallas_call(
        functools.partial(sums_kernel, truncation, n_wave, first_pair, last),
        in_specs=[SMEM, SMEM] + [VMEM] * (3 + len(shards) + len(earlier)),
        out_specs=VMEM,
        out_shape=out,
        scratch_shapes=[pltpu.VMEM((rows, columns), F32)] if last else [],
        compiler_params=PARAMS,
        name="legendre_sums",
    )(place, pair_lower, pick, limit, spec, *shards, *earlier)


def place_kernel(lat_dev, waves_ref, *refs):
    received_refs, (out_ref, rows_ref, held_ref) = refs[:-3], refs[-3:]
    count = waves_ref.shape[1]
    columns = out_ref.shape[2]
    base = 0
    for received_ref in received_refs:
        rows = received_ref.shape[0]

        def widen(d, carry):
            at = pl.multiple_of(d * PIECE, PIECE)
            rows_ref[pl.ds(at + base * 2 * lat_dev, PIECE), :] = received_ref[pl.ds(at, PIECE), :].astype(F32)
            return carry

        lax.fori_loop(0, rows // PIECE, widen, 0, unroll=8)
        many = rows // (2 * lat_dev)
        for h in range(2):
            for lat in range(lat_dev):
                taken = rows_ref[pl.ds(base * 2 * lat_dev + h * lat_dev + lat, many, stride=2 * lat_dev), :]
                at = 2 * base + h * many
                held_ref[at:at + many, lat * columns:(lat + 1) * columns] = taken.astype(BF)
        base += many
    tall = 256
    for m in range(0, count, tall):
        index = lax.broadcasted_iota(jnp.int32, (tall, count), 0) + m
        chosen = jnp.where(index == waves_ref[...], 1.0, 0.0).astype(BF)
        placed = jnp.dot(chosen, held_ref[...], preferred_element_type=F32).astype(BF)
        for lat in range(lat_dev):
            out_ref[lat, m:m + tall, :] = placed[:, lat * columns:(lat + 1) * columns]


def place_waves(waves, received, lat_dev):
    count = waves.shape[1]
    columns = received[0].shape[1]
    return pl.pallas_call(
        functools.partial(place_kernel, lat_dev),
        out_shape=jax.ShapeDtypeStruct((lat_dev, count, columns), BF),
        scratch_shapes=[
            pltpu.VMEM((lat_dev * count, columns), F32),
            pltpu.VMEM((count, lat_dev * columns), BF),
        ],
        compiler_params=PARAMS,
        name="place_waves",
    )(waves, *received)


def gather_ring(groups):
    n = lax.axis_size("fld")
    assert n == 8 and len(groups) == 2

    def up(x):
        return lax.ppermute(x, "fld", [(i, (i + 1) % n) for i in range(n)])

    def down(x):
        return lax.ppermute(x, "fld", [(i, (i - 1) % n) for i in range(n)])

    below, above = [[x] for x in groups], [[x] for x in groups]
    for step in range(n // 2):
        for g in range(2):
            if step < n // 2 - 1 or g == 0:
                below[g].append(up(below[g][-1]))
            if step < n // 2 - 1 or g == 1:
                above[g].append(down(above[g][-1]))
    return [[groups[g]] + above[g][1:] + below[g][:0:-1] for g in range(2)]


def on_device(spec_coeffs, legendre, pair_lower, slot_latitude, cycle_points):
    pairs, _, half_slots, columns = spec_coeffs.shape
    truncation = 2 * half_slots - 3
    n_wave = lax.axis_size("wave")
    lats = slot_latitude.shape[0]
    lat_dev = lats // n_wave
    group = pairs // 2
    place = jnp.stack([lax.axis_index("wave"), lax.axis_index("fld")]).astype(jnp.int32)
    shards = gather_ring(pack_table(jnp.transpose(legendre, (0, 1, 3, 2)), 2))
    pick, limit = row_order(place, slot_latitude.reshape(1, lats), cycle_points.reshape(1, lats // 2), lat_dev)
    rows = []
    for g in range(2):
        sums = legendre_sums(
            place, pair_lower, pick, limit, spec_coeffs, shards[g], rows, g * group, group, g == 1, n_wave, truncation
        )
        rows.append(sums)
    sent = rows[-1].reshape(n_wave, -1, columns)
    received = [lax.all_to_all(sent, "wave", split_axis=0, concat_axis=0, tiled=True).reshape(-1, columns)]
    lower = pair_lower.reshape(1, -1)
    waves = jnp.concatenate([lower, truncation - lower], axis=1)
    return place_waves(waves, received, lat_dev)


def solution(mesh):
    placed = (P("wave", None, None, "fld"), P("wave", None, None, "fld"), P(), P(), P())
    return jax.shard_map(
        on_device, mesh=mesh, in_specs=placed, out_specs=P("wave", None, "fld"), check_vma=False
    )
```

```python
import functools

import jax
import jax.numpy as jnp
from jax import lax
from jax.experimental import pallas as pl
from jax.experimental.pallas import tpu as pltpu
from jax.sharding import PartitionSpec as P

BF = jnp.bfloat16
F32 = jnp.float32
LANES = 128
ROWS = 16
PLAIN = 2
VMEM = pl.BlockSpec(memory_space=pltpu.VMEM)
SMEM = pl.BlockSpec(memory_space=pltpu.SMEM)
PIECE = 80
UNROLL = True
PARAMS = pltpu.CompilerParams(vmem_limit_bytes=24 * 1024 * 1024)


def pack_kernel(table_ref, *out_refs):
    pairs, _, rows, half_slots = table_ref.shape
    blocks = half_slots // LANES
    group = pairs // len(out_refs)
    lane = lax.broadcasted_iota(jnp.int32, (rows, LANES), 1)
    for g, out_ref in enumerate(out_refs):
        last = jnp.zeros((rows, LANES), F32)
        for i in range(group):
            for r in range(2):
                for b in range(blocks):
                    out_ref[(2 * i + r) * blocks + b] = table_ref[g * group + i, r, :, b * LANES:(b + 1) * LANES]
                tail = table_ref[g * group + i, r, :, half_slots - 1:half_slots].astype(F32)
                last = jnp.where(lane == 2 * i + r, tail, last)
        out_ref[2 * group * blocks] = last.astype(BF)


def pack_table(table, groups):
    pairs, _, rows, half_slots = table.shape
    assert half_slots % LANES == 1
    length = 2 * (pairs // groups) * (half_slots // LANES) + 1
    return pl.pallas_call(
        pack_kernel,
        in_specs=[VMEM],
        out_specs=[VMEM] * groups,
        out_shape=[jax.ShapeDtypeStruct((length, rows, LANES), BF)] * groups,
        compiler_params=PARAMS,
        name="pack_table",
    )(table)


def even_partner(z):
    return z + 1 - 2 * (z % 2)


def odd_partner(z, n):
    return (z + n - 1 + 2 * (z % 2)) % n


def held_order(z, n, first):
    partners = [even_partner, lambda i: odd_partner(i, n)]
    near, far = partners[first], partners[1 - first]
    pairs, via = [(z, near(z))], z
    for step in range(1, n // 2):
        origin, path = z, []
        for k in range(step):
            path.append(far if (step - k) % 2 else near)
        for move in path:
            origin = move(origin)
        pairs.append((origin, near(origin)))
    return [i for pair in pairs for i in pair]


def rows_kernel(lat_dev, place_ref, slots_ref, points_ref, *out_refs):
    pick_refs, limit_ref = out_refs[:-1], out_refs[-1]
    lats = slots_ref.shape[1]
    half = lats // 2
    n_wave = lats // lat_dev
    sent = lax.broadcasted_iota(jnp.int32, (lats, lats), 1)
    source = lax.rem(sent, n_wave) * lat_dev + sent // n_wave
    moved = jnp.where(lax.broadcasted_iota(jnp.int32, (lats, lats), 0) == source, 1.0, 0.0).astype(BF)
    slots = jnp.broadcast_to(slots_ref[...].astype(F32), (ROWS, lats)).astype(BF)
    slots = jnp.dot(slots, moved, preferred_element_type=F32)[:1].astype(jnp.int32)
    cycle = lax.rem(slots, half)
    index = lax.broadcasted_iota(jnp.int32, (lats, lats), 0)
    for first, pick_ref in enumerate(pick_refs):
        held = lax.rem(cycle, ROWS) + (slots // half) * half
        for at, z in enumerate(held_order(place_ref[1], half // ROWS, first)):
            held = held + jnp.where(cycle // ROWS == z, at * ROWS, 0)
        pick_ref[...] = jnp.where(index == held, 1.0, 0.0).T.astype(BF)
    index = lax.broadcasted_iota(jnp.int32, (half, lats), 0)
    points = jnp.where(index == cycle, 1.0, 0.0).T * points_ref[...].astype(F32)
    limit_ref[...] = jnp.broadcast_to(jnp.sum(points, axis=1, keepdims=True), limit_ref.shape)


def row_order(place, slots, points, lat_dev):
    lats = slots.shape[1]
    assert lats <= 256
    return pl.pallas_call(
        functools.partial(rows_kernel, lat_dev),
        in_specs=[SMEM, VMEM, VMEM],
        out_specs=[VMEM] * 3,
        out_shape=[jax.ShapeDtypeStruct((lats, lats), BF)] * 2 + [jax.ShapeDtypeStruct((lats, LANES), F32)],
        compiler_params=PARAMS,
        name="row_order",
    )(place, slots, points)


def sums_kernel(truncation, n_wave, first_pair, last_group, place_ref, lower_ref, pick_ref, limit_ref, spec_ref, *refs):
    shard_refs, earlier, out_ref = refs[:5], refs[5:-2] if last_group else (), refs[-2] if last_group else refs[-1]
    rows_ref = refs[-1]
    all_pairs, _, half_slots, columns = spec_ref.shape
    lat_dev = pick_ref.shape[0] // n_wave
    per_dev = rows_ref.shape[0] // n_wave
    group = per_dev // (2 * lat_dev)
    full = half_slots - 1
    blocks = full // LANES
    plain = PLAIN * LANES

    def block(b, g):
        length = shard_refs[0].shape[0]
        parts = [ref[b + at] for ref in shard_refs for at in range(0, ref.shape[0], length)]
        return jnp.concatenate(parts, axis=0)

    def step(i, carry):
        for g in range(1):
            local = i
            pair = local + first_pair
            q = lower_ref[place_ref[0] * all_pairs + pair]
            length = truncation + 1 - q
            begin = length + lax.rem(length, 2)
            tails = block(2 * group * blocks, g)
            sums = []
            for r in range(2):
                def owned(slot, coeffs, lower):
                    kept = slot < length if lower else (slot >= begin) & (slot <= begin + q)
                    return jnp.where(kept, coeffs, 0.0).astype(BF)

                table = [block((2 * i + r) * blocks + b, g) for b in range(blocks)]
                below = jnp.dot(
                    jnp.concatenate(table[:PLAIN], axis=1), spec_ref[pair, r, :plain, :], preferred_element_type=F32
                )
                coeffs = spec_ref[pair, r, plain:full, :].astype(F32)
                slot = 2 * (lax.broadcasted_iota(jnp.int32, coeffs.shape, 0) + plain) + r
                row = lax.broadcasted_iota(jnp.int32, (LANES, columns), 0)
                tail = jnp.where(row == 2 * i + r, spec_ref[pair, r, full:, :].astype(F32), 0.0)
                last = jnp.full((LANES, columns), 2 * full + r, jnp.int32)
                both = [
                    jnp.concatenate([owned(slot, coeffs, lower), owned(last, tail, lower)], axis=0)
                    for lower in (True, False)
                ]
                above = jnp.dot(
                    jnp.concatenate(table[PLAIN:] + [tails], axis=1),
                    jnp.concatenate(both, axis=1),
                    preferred_element_type=F32,
                )
                sums.append((above[:, :columns] + below, above[:, columns:]))
            north = jnp.concatenate([sums[0][h] + sums[1][h] for h in range(2)], axis=1)
            south = jnp.concatenate([sums[0][h] - sums[1][h] for h in range(2)], axis=1)
            fourier = jnp.concatenate([north, south], axis=0).astype(BF)
            picked = jnp.dot(pick_ref[...], fourier, preferred_element_type=F32)
            for h in range(2):
                wave = (q if h == 0 else truncation - q).astype(F32)
                kept = jnp.where(2.0 * wave < limit_ref[...], picked[:, h * columns:(h + 1) * columns], 0.0)
                for lat in range(lat_dev):
                    start = (2 * local + h) * lat_dev + lat
                    rows_ref[pl.ds(start, n_wave, stride=per_dev), :] = kept[lat * n_wave:(lat + 1) * n_wave]
        return carry

    lax.fori_loop(0, group, step, 0, unroll=UNROLL)

    def narrow(d, carry):
        at = pl.ds(pl.multiple_of(d * per_dev, per_dev), per_dev)
        parts = [ref[at, :] for ref in earlier + (rows_ref,)]
        sent = per_dev * len(parts)
        out_ref[pl.ds(pl.multiple_of(d * sent, sent), sent), :] = jnp.concatenate(parts, axis=0).astype(BF)
        return carry

    if last_group:
        lax.fori_loop(0, n_wave, narrow, 0, unroll=8)


def legendre_sums(place, pair_lower, pick, limit, spec, shards, earlier, first_pair, group, last, n_wave, truncation):
    columns = spec.shape[3]
    rows = 2 * group * pick.shape[0]
    if last:
        out = jax.ShapeDtypeStruct((rows * (1 + len(earlier)), columns), BF)
    else:
        out, earlier = jax.ShapeDtypeStruct((rows, columns), F32), []
    return pl.pallas_call(
        functools.partial(sums_kernel, truncation, n_wave, first_pair, last),
        in_specs=[SMEM, SMEM] + [VMEM] * (3 + len(shards) + len(earlier)),
        out_specs=VMEM,
        out_shape=out,
        scratch_shapes=[pltpu.VMEM((rows, columns), F32)] if last else [],
        compiler_params=PARAMS,
        name="legendre_sums",
    )(place, pair_lower, pick, limit, spec, *shards, *earlier)


def place_kernel(lat_dev, waves_ref, *refs):
    received_refs, (out_ref, rows_ref, held_ref) = refs[:-3], refs[-3:]
    count = waves_ref.shape[1]
    columns = out_ref.shape[2]
    base = 0
    for received_ref in received_refs:
        rows = received_ref.shape[0]

        def widen(d, carry):
            at = pl.multiple_of(d * PIECE, PIECE)
            rows_ref[pl.ds(at + base * 2 * lat_dev, PIECE), :] = received_ref[pl.ds(at, PIECE), :].astype(F32)
            return carry

        lax.fori_loop(0, rows // PIECE, widen, 0, unroll=8)
        many = rows // (2 * lat_dev)
        for h in range(2):
            for lat in range(lat_dev):
                taken = rows_ref[pl.ds(base * 2 * lat_dev + h * lat_dev + lat, many, stride=2 * lat_dev), :]
                at = 2 * base + h * many
                held_ref[at:at + many, lat * columns:(lat + 1) * columns] = taken.astype(BF)
        base += many
    tall = 256
    for m in range(0, count, tall):
        index = lax.broadcasted_iota(jnp.int32, (tall, count), 0) + m
        chosen = jnp.where(index == waves_ref[...], 1.0, 0.0).astype(BF)
        placed = jnp.dot(chosen, held_ref[...], preferred_element_type=F32).astype(BF)
        for lat in range(lat_dev):
            out_ref[lat, m:m + tall, :] = placed[:, lat * columns:(lat + 1) * columns]


def place_waves(waves, received, lat_dev):
    count = waves.shape[1]
    columns = received[0].shape[1]
    return pl.pallas_call(
        functools.partial(place_kernel, lat_dev),
        out_shape=jax.ShapeDtypeStruct((lat_dev, count, columns), BF),
        scratch_shapes=[
            pltpu.VMEM((lat_dev * count, columns), F32),
            pltpu.VMEM((count, lat_dev * columns), BF),
        ],
        compiler_params=PARAMS,
        name="place_waves",
    )(waves, *received)


def gather_table(groups):
    n = lax.axis_size("fld")
    kinds = [
        [(i, even_partner(i)) for i in range(n)],
        [(i, odd_partner(i, n)) for i in range(n)],
    ]
    held = [[x] for x in groups]
    for step in range(n // 2):
        for first, parts in enumerate(held):
            sent = jnp.concatenate(parts, axis=0) if step == 1 else parts[-1]
            parts.append(lax.ppermute(sent, "fld", kinds[(first + step) % 2]))
    return held


def on_device(spec_coeffs, legendre, pair_lower, slot_latitude, cycle_points):
    pairs, _, half_slots, columns = spec_coeffs.shape
    truncation = 2 * half_slots - 3
    n_wave = lax.axis_size("wave")
    lats = slot_latitude.shape[0]
    lat_dev = lats // n_wave
    group = pairs // 2
    place = jnp.stack([lax.axis_index("wave"), lax.axis_index("fld")]).astype(jnp.int32)
    shards = gather_table(pack_table(jnp.transpose(legendre, (0, 1, 3, 2)), 2))
    *picks, limit = row_order(place, slot_latitude.reshape(1, lats), cycle_points.reshape(1, lats // 2), lat_dev)
    rows = []
    for g in range(2):
        sums = legendre_sums(
            place, pair_lower, picks[g], limit, spec_coeffs, shards[g], rows, g * group, group, g == 1, n_wave, truncation
        )
        rows.append(sums)
    sent = rows[-1].reshape(n_wave, -1, columns)
    received = [lax.all_to_all(sent, "wave", split_axis=0, concat_axis=0, tiled=True).reshape(-1, columns)]
    lower = pair_lower.reshape(1, -1)
    waves = jnp.concatenate([lower, truncation - lower], axis=1)
    return place_waves(waves, received, lat_dev)


def solution(mesh):
    placed = (P("wave", None, None, "fld"), P("wave", None, None, "fld"), P(), P(), P())
    return jax.shard_map(
        on_device, mesh=mesh, in_specs=placed, out_specs=P("wave", None, "fld"), check_vma=False
    )
```

```python
import functools

import jax
import jax.numpy as jnp
from jax import lax
from jax.experimental import pallas as pl
from jax.experimental.pallas import tpu as pltpu
from jax.sharding import PartitionSpec as P

BF = jnp.bfloat16
F32 = jnp.float32
LANES = 128
ROWS = 16
PLAIN = 2
VMEM = pl.BlockSpec(memory_space=pltpu.VMEM)
SMEM = pl.BlockSpec(memory_space=pltpu.SMEM)
LEFT = 4
PARAMS = pltpu.CompilerParams(vmem_limit_bytes=24 * 1024 * 1024)


def pack_kernel(table_ref, *out_refs):
    pairs, _, rows, half_slots = table_ref.shape
    blocks = half_slots // LANES
    group = pairs // len(out_refs)
    lane = lax.broadcasted_iota(jnp.int32, (rows, LANES), 1)
    for g, out_ref in enumerate(out_refs):
        last = jnp.zeros((rows, LANES), F32)
        for i in range(group):
            for r in range(2):
                for b in range(blocks):
                    out_ref[(2 * i + r) * blocks + b] = table_ref[g * group + i, r, :, b * LANES:(b + 1) * LANES]
                tail = table_ref[g * group + i, r, :, half_slots - 1:half_slots].astype(F32)
                last = jnp.where(lane == 2 * i + r, tail, last)
        out_ref[2 * group * blocks] = last.astype(BF)


def pack_table(table, groups):
    pairs, _, rows, half_slots = table.shape
    assert half_slots % LANES == 1
    length = 2 * (pairs // groups) * (half_slots // LANES) + 1
    return pl.pallas_call(
        pack_kernel,
        in_specs=[VMEM],
        out_specs=[VMEM] * groups,
        out_shape=[jax.ShapeDtypeStruct((length, rows, LANES), BF)] * groups,
        compiler_params=PARAMS,
        name="pack_table",
    )(table)


def even_partner(z):
    return z + 1 - 2 * (z % 2)


def odd_partner(z, n):
    return (z + n - 1 + 2 * (z % 2)) % n


def held_order(z, n, first):
    partners = [even_partner, lambda i: odd_partner(i, n)]
    near, far = partners[first], partners[1 - first]
    pairs, via = [(z, near(z))], z
    for step in range(1, n // 2):
        origin, path = z, []
        for k in range(step):
            path.append(far if (step - k) % 2 else near)
        for move in path:
            origin = move(origin)
        pairs.append((origin, near(origin)))
    return [i for pair in pairs for i in pair]


def rows_kernel(lat_dev, place_ref, slots_ref, points_ref, *out_refs):
    pick_refs, limit_ref = out_refs[:-1], out_refs[-1]
    lats = slots_ref.shape[1]
    half = lats // 2
    n_wave = lats // lat_dev
    sent = lax.broadcasted_iota(jnp.int32, (lats, lats), 1)
    source = lax.rem(sent, n_wave) * lat_dev + sent // n_wave
    moved = jnp.where(lax.broadcasted_iota(jnp.int32, (lats, lats), 0) == source, 1.0, 0.0).astype(BF)
    slots = jnp.broadcast_to(slots_ref[...].astype(F32), (ROWS, lats)).astype(BF)
    slots = jnp.dot(slots, moved, preferred_element_type=F32)[:1].astype(jnp.int32)
    cycle = lax.rem(slots, half)
    index = lax.broadcasted_iota(jnp.int32, (lats, lats), 0)
    for first, pick_ref in enumerate(pick_refs):
        held = lax.rem(cycle, ROWS) + (slots // half) * half
        for at, z in enumerate(held_order(place_ref[1], half // ROWS, first)):
            held = held + jnp.where(cycle // ROWS == z, at * ROWS, 0)
        pick_ref[...] = jnp.where(index == held, 1.0, 0.0).T.astype(BF)
    index = lax.broadcasted_iota(jnp.int32, (half, lats), 0)
    points = jnp.where(index == cycle, 1.0, 0.0).T * points_ref[...].astype(F32)
    limit_ref[...] = jnp.broadcast_to(jnp.sum(points, axis=1, keepdims=True), limit_ref.shape)


def row_order(place, slots, points, lat_dev):
    lats = slots.shape[1]
    assert lats <= 256
    return pl.pallas_call(
        functools.partial(rows_kernel, lat_dev),
        in_specs=[SMEM, VMEM, VMEM],
        out_specs=[VMEM] * 3,
        out_shape=[jax.ShapeDtypeStruct((lats, lats), BF)] * 2 + [jax.ShapeDtypeStruct((lats, LANES), F32)],
        compiler_params=PARAMS,
        name="row_order",
    )(place, slots, points)


def sent_row(pair, h, lat, lat_dev):
    row = 2 * pair + h
    return lat * ROWS + row if row < ROWS else lat_dev * ROWS + lat * LEFT + row - ROWS


def sums_kernel(truncation, n_wave, first_pair, last_group, place_ref, lower_ref, pick_ref, limit_ref, spec_ref, *refs):
    shard_refs, earlier, out_ref = refs[:5], refs[5:-2] if last_group else (), refs[-2] if last_group else refs[-1]
    rows_ref = refs[-1]
    all_pairs, _, half_slots, columns = spec_ref.shape
    lat_dev = pick_ref.shape[0] // n_wave
    per_dev = rows_ref.shape[0] // n_wave
    group = all_pairs // 2
    full = half_slots - 1
    blocks = full // LANES
    plain = PLAIN * LANES

    def block(b):
        length = shard_refs[0].shape[0]
        parts = [ref[b + at] for ref in shard_refs for at in range(0, ref.shape[0], length)]
        return jnp.concatenate(parts, axis=0)

    def step(i):
        for pair in (i + first_pair,):
            q = lower_ref[place_ref[0] * all_pairs + pair]
            length = truncation + 1 - q
            begin = length + lax.rem(length, 2)
            tails = block(2 * group * blocks)
            sums = []
            for r in range(2):
                def owned(slot, coeffs, lower):
                    kept = slot < length if lower else (slot >= begin) & (slot <= begin + q)
                    return jnp.where(kept, coeffs, 0.0).astype(BF)

                table = [block((2 * i + r) * blocks + b) for b in range(blocks)]
                below = jnp.dot(
                    jnp.concatenate(table[:PLAIN], axis=1), spec_ref[pair, r, :plain, :], preferred_element_type=F32
                )
                coeffs = spec_ref[pair, r, plain:full, :].astype(F32)
                slot = 2 * (lax.broadcasted_iota(jnp.int32, coeffs.shape, 0) + plain) + r
                row = lax.broadcasted_iota(jnp.int32, (LANES, columns), 0)
                tail = jnp.where(row == 2 * i + r, spec_ref[pair, r, full:, :].astype(F32), 0.0)
                last = jnp.full((LANES, columns), 2 * full + r, jnp.int32)
                both = [
                    jnp.concatenate([owned(slot, coeffs, lower), owned(last, tail, lower)], axis=0)
                    for lower in (True, False)
                ]
                above = jnp.dot(
                    jnp.concatenate(table[PLAIN:] + [tails], axis=1),
                    jnp.concatenate(both, axis=1),
                    preferred_element_type=F32,
                )
                sums.append((above[:, :columns] + below, above[:, columns:]))
            north = jnp.concatenate([sums[0][h] + sums[1][h] for h in range(2)], axis=1)
            south = jnp.concatenate([sums[0][h] - sums[1][h] for h in range(2)], axis=1)
            fourier = jnp.concatenate([north, south], axis=0).astype(BF)
            picked = jnp.dot(pick_ref[...], fourier, preferred_element_type=F32)
            for h in range(2):
                wave = (q if h == 0 else truncation - q).astype(F32)
                kept = jnp.where(2.0 * wave < limit_ref[...], picked[:, h * columns:(h + 1) * columns], 0.0)
                for lat in range(lat_dev):
                    at = pl.ds(sent_row(pair, h, lat, lat_dev), n_wave, stride=per_dev)
                    rows_ref[at, :] = kept[lat * n_wave:(lat + 1) * n_wave]

    for i in range(group):
        step(i)

    def narrow(d, carry):
        base = pl.multiple_of(d * per_dev, per_dev)
        parts = []
        for at in range(0, per_dev, 8):
            there = 2 * group - at % ROWS if at < lat_dev * ROWS else 0
            rows = pl.ds(base + at, 8)
            if there <= 0:
                parts.append(rows_ref[rows, :])
            elif there >= 8:
                parts.append(earlier[0][rows, :])
            else:
                row = lax.broadcasted_iota(jnp.int32, (8, columns), 0)
                parts.append(jnp.where(row < there, earlier[0][rows, :], rows_ref[rows, :]))
        out_ref[pl.ds(base, per_dev), :] = jnp.concatenate(parts, axis=0).astype(BF)
        return carry

    if last_group:
        lax.fori_loop(0, n_wave, narrow, 0, unroll=16)


def legendre_sums(place, pair_lower, pick, limit, spec, shards, earlier, first_pair, group, last, n_wave, truncation):
    columns = spec.shape[3]
    rows = 4 * group * pick.shape[0]
    out = jax.ShapeDtypeStruct((rows, columns), BF if last else F32)
    return pl.pallas_call(
        functools.partial(sums_kernel, truncation, n_wave, first_pair, last),
        in_specs=[SMEM, SMEM] + [VMEM] * (3 + len(shards) + len(earlier)),
        out_specs=VMEM,
        out_shape=out,
        scratch_shapes=[pltpu.VMEM((rows, columns), F32)] if last else [],
        compiler_params=PARAMS,
        name="legendre_sums",
    )(place, pair_lower, pick, limit, spec, *shards, *earlier)


def place_kernel(waves_ref, received_ref, out_ref, rows_ref, left_ref, placed_ref, sems):
    lat_dev, count, columns = placed_ref.shape
    n_wave = received_ref.shape[0]
    main = n_wave * ROWS
    rows_ref[...] = received_ref[:, lat_dev * ROWS:, :].astype(F32).reshape(rows_ref.shape)
    for lat in range(lat_dev):
        for i in range(LEFT):
            rows = rows_ref[pl.ds(lat * LEFT + i, n_wave, stride=lat_dev * LEFT), :]
            left_ref[i * n_wave:(i + 1) * n_wave, lat * columns:(lat + 1) * columns] = rows.astype(BF)
    held = [received_ref[:, lat * ROWS:(lat + 1) * ROWS, :].reshape(main, columns) for lat in range(lat_dev)]
    held = jnp.concatenate([jnp.concatenate(held, axis=1), left_ref[...]], axis=0)
    tall = count // 4
    copies = []
    for n in range(4):
        index = lax.broadcasted_iota(jnp.int32, (tall, count), 0) + n * tall
        chosen = jnp.where(index == waves_ref[...], 1.0, 0.0).astype(BF)
        placed = jnp.dot(chosen, held, preferred_element_type=F32).astype(BF)
        at = pl.ds(n * tall, tall)
        for lat in range(lat_dev):
            placed_ref[lat, n * tall:(n + 1) * tall, :] = placed[:, lat * columns:(lat + 1) * columns]
        copies.append(pltpu.make_async_copy(placed_ref.at[:, at, :], out_ref.at[:, at, :], sems.at[n]))
        copies[-1].start()
    for copy in copies:
        copy.wait()


def place_waves(waves, received, lat_dev):
    count = waves.shape[1]
    n_wave, _, columns = received.shape
    return pl.pallas_call(
        place_kernel,
        out_specs=pl.BlockSpec(memory_space=pltpu.HBM),
        out_shape=jax.ShapeDtypeStruct((lat_dev, count, columns), BF),
        scratch_shapes=[
            pltpu.VMEM((n_wave * lat_dev * LEFT, columns), F32),
            pltpu.VMEM((n_wave * LEFT, lat_dev * columns), BF),
            pltpu.VMEM((lat_dev, count, columns), BF),
            pltpu.SemaphoreType.DMA((4,)),
        ],
        compiler_params=PARAMS,
        name="place_waves",
    )(waves, received)


def gather_table(groups):
    n = lax.axis_size("fld")
    kinds = [
        [(i, even_partner(i)) for i in range(n)],
        [(i, odd_partner(i, n)) for i in range(n)],
    ]
    held = [[x] for x in groups]
    for step in range(n // 2):
        for first, parts in enumerate(held):
            sent = jnp.concatenate(parts, axis=0) if step == 1 else parts[-1]
            parts.append(lax.ppermute(sent, "fld", kinds[(first + step) % 2]))
    return held


def on_device(spec_coeffs, legendre, pair_lower, slot_latitude, cycle_points):
    pairs, _, half_slots, columns = spec_coeffs.shape
    truncation = 2 * half_slots - 3
    n_wave = lax.axis_size("wave")
    lats = slot_latitude.shape[0]
    lat_dev = lats // n_wave
    group = pairs // 2
    place = jnp.stack([lax.axis_index("wave"), lax.axis_index("fld")]).astype(jnp.int32)
    shards = gather_table(pack_table(jnp.transpose(legendre, (0, 1, 3, 2)), 2))
    *picks, limit = row_order(place, slot_latitude.reshape(1, lats), cycle_points.reshape(1, lats // 2), lat_dev)
    assert 2 * pairs == ROWS + LEFT and lat_dev * LEFT == ROWS
    rows = []
    for g in range(2):
        sums = legendre_sums(
            place, pair_lower, picks[g], limit, spec_coeffs, shards[g], rows, g * group, group, g == 1, n_wave, truncation
        )
        rows.append(sums)
    sent, lower = lax.optimization_barrier((rows[-1].reshape(n_wave, -1, columns), pair_lower))
    received = lax.all_to_all(sent, "wave", split_axis=0, concat_axis=0, tiled=True)
    lower = lower.reshape(n_wave, pairs)
    held = jnp.stack([lower, truncation - lower], axis=2).reshape(n_wave, 2 * pairs)
    waves = jnp.concatenate([held[:, :ROWS].reshape(-1), held[:, ROWS:].T.reshape(-1)]).reshape(1, truncation + 1)
    return place_waves(waves, received, lat_dev)


def solution(mesh):
    placed = (P("wave", None, None, "fld"), P("wave", None, None, "fld"), P(), P(), P())
    return jax.shard_map(
        on_device, mesh=mesh, in_specs=placed, out_specs=P("wave", None, "fld"), check_vma=False
    )
```

```python
import functools

import jax
import jax.numpy as jnp
from jax import lax
from jax.experimental import pallas as pl
from jax.experimental.pallas import tpu as pltpu
from jax.sharding import PartitionSpec as P

BF = jnp.bfloat16
F32 = jnp.float32
LANES = 128
ROWS = 16
PLAIN = 2
VMEM = pl.BlockSpec(memory_space=pltpu.VMEM)
SMEM = pl.BlockSpec(memory_space=pltpu.SMEM)
LEFT = 4
PARAMS = pltpu.CompilerParams(vmem_limit_bytes=24 * 1024 * 1024)


def pack_kernel(first, table_ref, out_ref, held_ref, sem):
    group, _, rows, half_slots = held_ref.shape
    blocks = half_slots // LANES
    fetch = pltpu.make_async_copy(table_ref.at[pl.ds(first, group)], held_ref, sem)
    fetch.start()
    fetch.wait()
    lane = lax.broadcasted_iota(jnp.int32, (rows, LANES), 1)
    last = jnp.zeros((rows, LANES), F32)
    for i in range(group):
        for r in range(2):
            for b in range(blocks):
                out_ref[(2 * i + r) * blocks + b] = held_ref[i, r, :, b * LANES:(b + 1) * LANES]
            tail = held_ref[i, r, :, half_slots - 1:half_slots].astype(F32)
            last = jnp.where(lane == 2 * i + r, tail, last)
    out_ref[2 * group * blocks] = last.astype(BF)


def pack_table(table, groups):
    pairs, _, rows, half_slots = table.shape
    assert half_slots % LANES == 1
    group = pairs // groups
    length = 2 * group * (half_slots // LANES) + 1
    return [
        pl.pallas_call(
            functools.partial(pack_kernel, g * group),
            in_specs=[pl.BlockSpec(memory_space=pltpu.HBM)],
            out_specs=VMEM,
            out_shape=jax.ShapeDtypeStruct((length, rows, LANES), BF),
            scratch_shapes=[pltpu.VMEM((group, 2, rows, half_slots), BF), pltpu.SemaphoreType.DMA],
            compiler_params=pltpu.CompilerParams(vmem_limit_bytes=60 * 1024 * 1024),
            name="pack_table",
        )(table)
        for g in range(groups)
    ]


def even_partner(z):
    return z + 1 - 2 * (z % 2)


def odd_partner(z, n):
    return (z + n - 1 + 2 * (z % 2)) % n


def held_order(z, n, first):
    partners = [even_partner, lambda i: odd_partner(i, n)]
    near, far = partners[first], partners[1 - first]
    pairs, via = [(z, near(z))], z
    for step in range(1, n // 2):
        origin, path = z, []
        for k in range(step):
            path.append(far if (step - k) % 2 else near)
        for move in path:
            origin = move(origin)
        pairs.append((origin, near(origin)))
    return [i for pair in pairs for i in pair]


def rows_kernel(lat_dev, place_ref, slots_ref, points_ref, *out_refs):
    pick_refs, limit_ref = out_refs[:-1], out_refs[-1]
    lats = slots_ref.shape[1]
    half = lats // 2
    n_wave = lats // lat_dev
    sent = lax.broadcasted_iota(jnp.int32, (lats, lats), 1)
    source = lax.rem(sent, n_wave) * lat_dev + sent // n_wave
    moved = jnp.where(lax.broadcasted_iota(jnp.int32, (lats, lats), 0) == source, 1.0, 0.0).astype(BF)
    slots = jnp.broadcast_to(slots_ref[...].astype(F32), (ROWS, lats)).astype(BF)
    slots = jnp.dot(slots, moved, preferred_element_type=F32)[:1].astype(jnp.int32)
    cycle = lax.rem(slots, half)
    index = lax.broadcasted_iota(jnp.int32, (lats, lats), 0)
    for first, pick_ref in enumerate(pick_refs):
        held = lax.rem(cycle, ROWS) + (slots // half) * half
        for at, z in enumerate(held_order(place_ref[1], half // ROWS, first)):
            held = held + jnp.where(cycle // ROWS == z, at * ROWS, 0)
        pick_ref[...] = jnp.where(index == held, 1.0, 0.0).T.astype(BF)
    index = lax.broadcasted_iota(jnp.int32, (half, lats), 0)
    points = jnp.where(index == cycle, 1.0, 0.0).T * points_ref[...].astype(F32)
    limit_ref[...] = jnp.broadcast_to(jnp.sum(points, axis=1, keepdims=True), limit_ref.shape)


def row_order(place, slots, points, lat_dev):
    lats = slots.shape[1]
    assert lats <= 256
    return pl.pallas_call(
        functools.partial(rows_kernel, lat_dev),
        in_specs=[SMEM, VMEM, VMEM],
        out_specs=[VMEM] * 3,
        out_shape=[jax.ShapeDtypeStruct((lats, lats), BF)] * 2 + [jax.ShapeDtypeStruct((lats, LANES), F32)],
        compiler_params=PARAMS,
        name="row_order",
    )(place, slots, points)


def sent_row(pair, h, lat, lat_dev):
    row = 2 * pair + h
    return lat * ROWS + row if row < ROWS else lat_dev * ROWS + lat * LEFT + row - ROWS


def sums_kernel(truncation, n_wave, first_pair, last_group, place_ref, lower_ref, pick_ref, limit_ref, spec_ref, *refs):
    shard_refs, earlier, out_ref = refs[:5], refs[5:-2] if last_group else (), refs[-2] if last_group else refs[-1]
    rows_ref = refs[-1]
    all_pairs, _, half_slots, columns = spec_ref.shape
    lat_dev = pick_ref.shape[0] // n_wave
    per_dev = rows_ref.shape[0] // n_wave
    group = all_pairs // 2
    full = half_slots - 1
    blocks = full // LANES
    plain = PLAIN * LANES

    def block(b):
        length = shard_refs[0].shape[0]
        parts = [ref[b + at] for ref in shard_refs for at in range(0, ref.shape[0], length)]
        return jnp.concatenate(parts, axis=0)

    def step(i):
        for pair in (i + first_pair,):
            q = lower_ref[place_ref[0] * all_pairs + pair]
            length = truncation + 1 - q
            begin = length + lax.rem(length, 2)
            tails = block(2 * group * blocks)
            sums = []
            for r in range(2):
                def owned(slot, coeffs, lower):
                    kept = slot < length if lower else (slot >= begin) & (slot <= begin + q)
                    return jnp.where(kept, coeffs, 0.0).astype(BF)

                table = [block((2 * i + r) * blocks + b) for b in range(blocks)]
                below = jnp.dot(
                    jnp.concatenate(table[:PLAIN], axis=1), spec_ref[pair, r, :plain, :], preferred_element_type=F32
                )
                coeffs = spec_ref[pair, r, plain:full, :].astype(F32)
                slot = 2 * (lax.broadcasted_iota(jnp.int32, coeffs.shape, 0) + plain) + r
                row = lax.broadcasted_iota(jnp.int32, (LANES, columns), 0)
                tail = jnp.where(row == 2 * i + r, spec_ref[pair, r, full:, :].astype(F32), 0.0)
                last = jnp.full((LANES, columns), 2 * full + r, jnp.int32)
                both = [
                    jnp.concatenate([owned(slot, coeffs, lower), owned(last, tail, lower)], axis=0)
                    for lower in (True, False)
                ]
                above = jnp.dot(
                    jnp.concatenate(table[PLAIN:] + [tails], axis=1),
                    jnp.concatenate(both, axis=1),
                    preferred_element_type=F32,
                )
                sums.append((above[:, :columns] + below, above[:, columns:]))
            north = jnp.concatenate([sums[0][h] + sums[1][h] for h in range(2)], axis=1)
            south = jnp.concatenate([sums[0][h] - sums[1][h] for h in range(2)], axis=1)
            fourier = jnp.concatenate([north, south], axis=0).astype(BF)
            picked = jnp.dot(pick_ref[...], fourier, preferred_element_type=F32)
            for h in range(2):
                wave = (q if h == 0 else truncation - q).astype(F32)
                kept = jnp.where(2.0 * wave < limit_ref[...], picked[:, h * columns:(h + 1) * columns], 0.0)
                for lat in range(lat_dev):
                    at = pl.ds(sent_row(pair, h, lat, lat_dev), n_wave, stride=per_dev)
                    rows_ref[at, :] = kept[lat * n_wave:(lat + 1) * n_wave]

    for i in range(group):
        step(i)

    def narrow(d, carry):
        base = pl.multiple_of(d * per_dev, per_dev)
        parts = []
        for at in range(0, per_dev, 8):
            there = 2 * group - at % ROWS if at < lat_dev * ROWS else 0
            rows = pl.ds(base + at, 8)
            if there <= 0:
                parts.append(rows_ref[rows, :])
            elif there >= 8:
                parts.append(earlier[0][rows, :])
            else:
                row = lax.broadcasted_iota(jnp.int32, (8, columns), 0)
                parts.append(jnp.where(row < there, earlier[0][rows, :], rows_ref[rows, :]))
        out_ref[pl.ds(base, per_dev), :] = jnp.concatenate(parts, axis=0).astype(BF)
        return carry

    if last_group:
        lax.fori_loop(0, n_wave, narrow, 0, unroll=16)


def legendre_sums(place, pair_lower, pick, limit, spec, shards, earlier, first_pair, group, last, n_wave, truncation):
    columns = spec.shape[3]
    rows = 4 * group * pick.shape[0]
    out = jax.ShapeDtypeStruct((rows, columns), BF if last else F32)
    return pl.pallas_call(
        functools.partial(sums_kernel, truncation, n_wave, first_pair, last),
        in_specs=[SMEM, SMEM] + [VMEM] * (3 + len(shards) + len(earlier)),
        out_specs=VMEM,
        out_shape=out,
        scratch_shapes=[pltpu.VMEM((rows, columns), F32)] if last else [],
        compiler_params=PARAMS,
        name="legendre_sums",
    )(place, pair_lower, pick, limit, spec, *shards, *earlier)


def place_kernel(waves_ref, received_ref, out_ref, rows_ref, left_ref, placed_ref, sems):
    lat_dev, count, columns = placed_ref.shape
    n_wave = received_ref.shape[0]
    main = n_wave * ROWS
    rows_ref[...] = received_ref[:, lat_dev * ROWS:, :].astype(F32).reshape(rows_ref.shape)
    for lat in range(lat_dev):
        for i in range(LEFT):
            rows = rows_ref[pl.ds(lat * LEFT + i, n_wave, stride=lat_dev * LEFT), :]
            left_ref[i * n_wave:(i + 1) * n_wave, lat * columns:(lat + 1) * columns] = rows.astype(BF)
    held = [received_ref[:, lat * ROWS:(lat + 1) * ROWS, :].reshape(main, columns) for lat in range(lat_dev)]
    held = jnp.concatenate([jnp.concatenate(held, axis=1), left_ref[...]], axis=0)
    tall = count // 4
    copies = []
    for n in range(4):
        index = lax.broadcasted_iota(jnp.int32, (tall, count), 0) + n * tall
        chosen = jnp.where(index == waves_ref[...], 1.0, 0.0).astype(BF)
        placed = jnp.dot(chosen, held, preferred_element_type=F32).astype(BF)
        at = pl.ds(n * tall, tall)
        for lat in range(lat_dev):
            placed_ref[lat, n * tall:(n + 1) * tall, :] = placed[:, lat * columns:(lat + 1) * columns]
        copies.append(pltpu.make_async_copy(placed_ref.at[:, at, :], out_ref.at[:, at, :], sems.at[n]))
        copies[-1].start()
    for copy in copies:
        copy.wait()


def place_waves(waves, received, lat_dev):
    count = waves.shape[1]
    n_wave, _, columns = received.shape
    return pl.pallas_call(
        place_kernel,
        out_specs=pl.BlockSpec(memory_space=pltpu.HBM),
        out_shape=jax.ShapeDtypeStruct((lat_dev, count, columns), BF),
        scratch_shapes=[
            pltpu.VMEM((n_wave * lat_dev * LEFT, columns), F32),
            pltpu.VMEM((n_wave * LEFT, lat_dev * columns), BF),
            pltpu.VMEM((lat_dev, count, columns), BF),
            pltpu.SemaphoreType.DMA((4,)),
        ],
        compiler_params=PARAMS,
        name="place_waves",
    )(waves, received)


def gather_table(groups):
    n = lax.axis_size("fld")
    kinds = [
        [(i, even_partner(i)) for i in range(n)],
        [(i, odd_partner(i, n)) for i in range(n)],
    ]
    held = [[x] for x in groups]
    for step in range(n // 2):
        for first, parts in enumerate(held):
            sent = jnp.concatenate(parts, axis=0) if step == 1 else parts[-1]
            parts.append(lax.ppermute(sent, "fld", kinds[(first + step) % 2]))
    return held


def on_device(spec_coeffs, legendre, pair_lower, slot_latitude, cycle_points):
    pairs, _, half_slots, columns = spec_coeffs.shape
    truncation = 2 * half_slots - 3
    n_wave = lax.axis_size("wave")
    lats = slot_latitude.shape[0]
    lat_dev = lats // n_wave
    group = pairs // 2
    place = jnp.stack([lax.axis_index("wave"), lax.axis_index("fld")]).astype(jnp.int32)
    shards = gather_table(pack_table(jnp.transpose(legendre, (0, 1, 3, 2)), 2))
    *picks, limit = row_order(place, slot_latitude.reshape(1, lats), cycle_points.reshape(1, lats // 2), lat_dev)
    assert 2 * pairs == ROWS + LEFT and lat_dev * LEFT == ROWS
    rows = []
    for g in range(2):
        sums = legendre_sums(
            place, pair_lower, picks[g], limit, spec_coeffs, shards[g], rows, g * group, group, g == 1, n_wave, truncation
        )
        rows.append(sums)
    sent, lower = lax.optimization_barrier((rows[-1].reshape(n_wave, -1, columns), pair_lower))
    received = lax.all_to_all(sent, "wave", split_axis=0, concat_axis=0, tiled=True)
    lower = lower.reshape(n_wave, pairs)
    held = jnp.stack([lower, truncation - lower], axis=2).reshape(n_wave, 2 * pairs)
    waves = jnp.concatenate([held[:, :ROWS].reshape(-1), held[:, ROWS:].T.reshape(-1)]).reshape(1, truncation + 1)
    return place_waves(waves, received, lat_dev)


def solution(mesh):
    placed = (P("wave", None, None, "fld"), P("wave", None, None, "fld"), P(), P(), P())
    return jax.shard_map(
        on_device, mesh=mesh, in_specs=placed, out_specs=P("wave", None, "fld"), check_vma=False
    )
```

```python
import functools

import jax
import jax.numpy as jnp
from jax import lax
from jax.experimental import pallas as pl
from jax.experimental.pallas import tpu as pltpu
from jax.sharding import PartitionSpec as P

BF = jnp.bfloat16
F32 = jnp.float32
LANES = 128
ROWS = 16
PLAIN = 2
VMEM = pl.BlockSpec(memory_space=pltpu.VMEM)
SMEM = pl.BlockSpec(memory_space=pltpu.SMEM)
LEFT = 4
PARAMS = pltpu.CompilerParams(vmem_limit_bytes=24 * 1024 * 1024)


def pack_kernel(table_ref, *out_refs):
    pairs, _, rows, half_slots = table_ref.shape
    blocks = half_slots // LANES
    group = pairs // len(out_refs)
    lane = lax.broadcasted_iota(jnp.int32, (rows, LANES), 1)
    for g, out_ref in enumerate(out_refs):
        last = jnp.zeros((rows, LANES), F32)
        for i in range(group):
            for r in range(2):
                for b in range(blocks):
                    out_ref[(2 * i + r) * blocks + b] = table_ref[g * group + i, r, :, b * LANES:(b + 1) * LANES]
                tail = table_ref[g * group + i, r, :, half_slots - 1:half_slots].astype(F32)
                last = jnp.where(lane == 2 * i + r, tail, last)
        out_ref[2 * group * blocks] = last.astype(BF)


def pack_table(table, groups):
    pairs, _, rows, half_slots = table.shape
    assert half_slots % LANES == 1
    length = 2 * (pairs // groups) * (half_slots // LANES) + 1
    return pl.pallas_call(
        pack_kernel,
        in_specs=[VMEM],
        out_specs=[VMEM] * groups,
        out_shape=[jax.ShapeDtypeStruct((length, rows, LANES), BF)] * groups,
        compiler_params=PARAMS,
        name="pack_table",
    )(table)


def even_partner(z):
    return z + 1 - 2 * (z % 2)


def odd_partner(z, n):
    return (z + n - 1 + 2 * (z % 2)) % n


def held_order(z, n, first):
    partners = [even_partner, lambda i: odd_partner(i, n)]
    near, far = partners[first], partners[1 - first]
    pairs, via = [(z, near(z))], z
    for step in range(1, n // 2):
        origin, path = z, []
        for k in range(step):
            path.append(far if (step - k) % 2 else near)
        for move in path:
            origin = move(origin)
        pairs.append((origin, near(origin)))
    return [i for pair in pairs for i in pair]


def rows_kernel(lat_dev, place_ref, slots_ref, points_ref, *out_refs):
    pick_refs, limit_ref = out_refs[:-1], out_refs[-1]
    lats = slots_ref.shape[1]
    half = lats // 2
    n_wave = lats // lat_dev
    sent = lax.broadcasted_iota(jnp.int32, (lats, lats), 1)
    source = lax.rem(sent, n_wave) * lat_dev + sent // n_wave
    moved = jnp.where(lax.broadcasted_iota(jnp.int32, (lats, lats), 0) == source, 1.0, 0.0).astype(BF)
    slots = jnp.broadcast_to(slots_ref[...].astype(F32), (ROWS, lats)).astype(BF)
    slots = jnp.dot(slots, moved, preferred_element_type=F32)[:1].astype(jnp.int32)
    cycle = lax.rem(slots, half)
    index = lax.broadcasted_iota(jnp.int32, (lats, lats), 0)
    for first, pick_ref in enumerate(pick_refs):
        held = lax.rem(cycle, ROWS) + (slots // half) * half
        for at, z in enumerate(held_order(place_ref[1], half // ROWS, first)):
            held = held + jnp.where(cycle // ROWS == z, at * ROWS, 0)
        pick_ref[...] = jnp.where(index == held, 1.0, 0.0).T.astype(BF)
    index = lax.broadcasted_iota(jnp.int32, (half, lats), 0)
    points = jnp.where(index == cycle, 1.0, 0.0).T * points_ref[...].astype(F32)
    limit_ref[...] = jnp.broadcast_to(jnp.sum(points, axis=1, keepdims=True), limit_ref.shape)


def row_order(place, slots, points, lat_dev):
    lats = slots.shape[1]
    assert lats <= 256
    return pl.pallas_call(
        functools.partial(rows_kernel, lat_dev),
        in_specs=[SMEM, VMEM, VMEM],
        out_specs=[VMEM] * 3,
        out_shape=[jax.ShapeDtypeStruct((lats, lats), BF)] * 2 + [jax.ShapeDtypeStruct((lats, LANES), F32)],
        compiler_params=PARAMS,
        name="row_order",
    )(place, slots, points)


def sent_row(pair, h, lat, lat_dev):
    row = 2 * pair + h
    return lat * ROWS + row if row < ROWS else lat_dev * ROWS + lat * LEFT + row - ROWS


def sums_kernel(truncation, n_wave, first_pair, last_group, place_ref, lower_ref, pick_ref, limit_ref, spec_ref, *refs):
    shard_refs, earlier, out_ref = refs[:5], refs[5:-2] if last_group else (), refs[-2] if last_group else refs[-1]
    rows_ref = refs[-1]
    all_pairs, _, half_slots, columns = spec_ref.shape
    lat_dev = pick_ref.shape[0] // n_wave
    per_dev = rows_ref.shape[0] // n_wave
    group = all_pairs // 2
    full = half_slots - 1
    blocks = full // LANES
    plain = PLAIN * LANES

    def block(b):
        length = shard_refs[0].shape[0]
        parts = [ref[b + at] for ref in shard_refs for at in range(0, ref.shape[0], length)]
        return jnp.concatenate(parts, axis=0)

    def step(i):
        for pair in (i + first_pair,):
            q = lower_ref[place_ref[0] * all_pairs + pair]
            length = truncation + 1 - q
            begin = length + lax.rem(length, 2)
            tails = block(2 * group * blocks)
            sums = []
            first = [
                jnp.concatenate([block((2 * i + r) * blocks + b) for b in range(PLAIN)], axis=1) for r in range(2)
            ]
            plain_coeffs = jnp.concatenate([spec_ref[pair, r, :plain, :] for r in range(2)], axis=1)
            below = jnp.dot(jnp.concatenate(first, axis=0), plain_coeffs, preferred_element_type=F32)
            below = [below[:first[0].shape[0], :columns], below[first[0].shape[0]:, columns:]]
            for r in range(2):
                def owned(slot, coeffs, lower):
                    kept = slot < length if lower else (slot >= begin) & (slot <= begin + q)
                    return jnp.where(kept, coeffs, 0.0).astype(BF)

                table = [block((2 * i + r) * blocks + b) for b in range(PLAIN, blocks)]
                coeffs = spec_ref[pair, r, plain:full, :].astype(F32)
                slot = 2 * (lax.broadcasted_iota(jnp.int32, coeffs.shape, 0) + plain) + r
                row = lax.broadcasted_iota(jnp.int32, (LANES, columns), 0)
                tail = jnp.where(row == 2 * i + r, spec_ref[pair, r, full:, :].astype(F32), 0.0)
                last = jnp.full((LANES, columns), 2 * full + r, jnp.int32)
                both = [
                    jnp.concatenate([owned(slot, coeffs, lower), owned(last, tail, lower)], axis=0)
                    for lower in (True, False)
                ]
                above = jnp.dot(
                    jnp.concatenate(table + [tails], axis=1),
                    jnp.concatenate(both, axis=1),
                    preferred_element_type=F32,
                )
                sums.append((above[:, :columns] + below[r], above[:, columns:]))
            north = jnp.concatenate([sums[0][h] + sums[1][h] for h in range(2)], axis=1)
            south = jnp.concatenate([sums[0][h] - sums[1][h] for h in range(2)], axis=1)
            fourier = jnp.concatenate([north, south], axis=0).astype(BF)
            picked = jnp.dot(pick_ref[...], fourier, preferred_element_type=F32)
            for h in range(2):
                wave = (q if h == 0 else truncation - q).astype(F32)
                kept = jnp.where(2.0 * wave < limit_ref[...], picked[:, h * columns:(h + 1) * columns], 0.0)
                for lat in range(lat_dev):
                    at = pl.ds(sent_row(pair, h, lat, lat_dev), n_wave, stride=per_dev)
                    rows_ref[at, :] = kept[lat * n_wave:(lat + 1) * n_wave]

    for i in range(group):
        step(i)

    def narrow(d, carry):
        base = pl.multiple_of(d * per_dev, per_dev)
        parts = []
        for at in range(0, per_dev, 8):
            there = 2 * group - at % ROWS if at < lat_dev * ROWS else 0
            rows = pl.ds(base + at, 8)
            if there <= 0:
                parts.append(rows_ref[rows, :])
            elif there >= 8:
                parts.append(earlier[0][rows, :])
            else:
                row = lax.broadcasted_iota(jnp.int32, (8, columns), 0)
                parts.append(jnp.where(row < there, earlier[0][rows, :], rows_ref[rows, :]))
        out_ref[pl.ds(base, per_dev), :] = jnp.concatenate(parts, axis=0).astype(BF)
        return carry

    if last_group:
        lax.fori_loop(0, n_wave, narrow, 0, unroll=16)


def legendre_sums(place, pair_lower, pick, limit, spec, shards, earlier, first_pair, group, last, n_wave, truncation):
    columns = spec.shape[3]
    rows = 4 * group * pick.shape[0]
    out = jax.ShapeDtypeStruct((rows, columns), BF if last else F32)
    return pl.pallas_call(
        functools.partial(sums_kernel, truncation, n_wave, first_pair, last),
        in_specs=[SMEM, SMEM] + [VMEM] * (3 + len(shards) + len(earlier)),
        out_specs=VMEM,
        out_shape=out,
        scratch_shapes=[pltpu.VMEM((rows, columns), F32)] if last else [],
        compiler_params=PARAMS,
        name="legendre_sums",
    )(place, pair_lower, pick, limit, spec, *shards, *earlier)


def place_kernel(waves_ref, received_ref, out_ref, rows_ref, left_ref, placed_ref, sems):
    lat_dev, count, columns = placed_ref.shape
    n_wave = received_ref.shape[0]
    main = n_wave * ROWS
    rows_ref[...] = received_ref[:, lat_dev * ROWS:, :].astype(F32).reshape(rows_ref.shape)
    for lat in range(lat_dev):
        for i in range(LEFT):
            rows = rows_ref[pl.ds(lat * LEFT + i, n_wave, stride=lat_dev * LEFT), :]
            left_ref[i * n_wave:(i + 1) * n_wave, lat * columns:(lat + 1) * columns] = rows.astype(BF)
    held = [received_ref[:, lat * ROWS:(lat + 1) * ROWS, :].reshape(main, columns) for lat in range(lat_dev)]
    held = jnp.concatenate([jnp.concatenate(held, axis=1), left_ref[...]], axis=0)
    tall = count // 4
    copies = []
    for n in range(4):
        index = lax.broadcasted_iota(jnp.int32, (tall, count), 0) + n * tall
        chosen = jnp.where(index == waves_ref[...], 1.0, 0.0).astype(BF)
        placed = jnp.dot(chosen, held, preferred_element_type=F32).astype(BF)
        at = pl.ds(n * tall, tall)
        for lat in range(lat_dev):
            placed_ref[lat, n * tall:(n + 1) * tall, :] = placed[:, lat * columns:(lat + 1) * columns]
        copies.append(pltpu.make_async_copy(placed_ref.at[:, at, :], out_ref.at[:, at, :], sems.at[n]))
        copies[-1].start()
    for copy in copies:
        copy.wait()


def place_waves(waves, received, lat_dev):
    count = waves.shape[1]
    n_wave, _, columns = received.shape
    return pl.pallas_call(
        place_kernel,
        out_specs=pl.BlockSpec(memory_space=pltpu.HBM),
        out_shape=jax.ShapeDtypeStruct((lat_dev, count, columns), BF),
        scratch_shapes=[
            pltpu.VMEM((n_wave * lat_dev * LEFT, columns), F32),
            pltpu.VMEM((n_wave * LEFT, lat_dev * columns), BF),
            pltpu.VMEM((lat_dev, count, columns), BF),
            pltpu.SemaphoreType.DMA((4,)),
        ],
        compiler_params=PARAMS,
        name="place_waves",
    )(waves, received)


def gather_table(groups):
    n = lax.axis_size("fld")
    kinds = [
        [(i, even_partner(i)) for i in range(n)],
        [(i, odd_partner(i, n)) for i in range(n)],
    ]
    held = [[x] for x in groups]
    for step in range(n // 2):
        for first, parts in enumerate(held):
            sent = jnp.concatenate(parts, axis=0) if step == 1 else parts[-1]
            parts.append(lax.ppermute(sent, "fld", kinds[(first + step) % 2]))
    return held


def on_device(spec_coeffs, legendre, pair_lower, slot_latitude, cycle_points):
    pairs, _, half_slots, columns = spec_coeffs.shape
    truncation = 2 * half_slots - 3
    n_wave = lax.axis_size("wave")
    lats = slot_latitude.shape[0]
    lat_dev = lats // n_wave
    group = pairs // 2
    place = jnp.stack([lax.axis_index("wave"), lax.axis_index("fld")]).astype(jnp.int32)
    shards = gather_table(pack_table(jnp.transpose(legendre, (0, 1, 3, 2)), 2))
    *picks, limit = row_order(place, slot_latitude.reshape(1, lats), cycle_points.reshape(1, lats // 2), lat_dev)
    assert 2 * pairs == ROWS + LEFT and lat_dev * LEFT == ROWS
    rows = []
    for g in range(2):
        sums = legendre_sums(
            place, pair_lower, picks[g], limit, spec_coeffs, shards[g], rows, g * group, group, g == 1, n_wave, truncation
        )
        rows.append(sums)
    sent, lower = lax.optimization_barrier((rows[-1].reshape(n_wave, -1, columns), pair_lower))
    received = lax.all_to_all(sent, "wave", split_axis=0, concat_axis=0, tiled=True)
    lower = lower.reshape(n_wave, pairs)
    held = jnp.stack([lower, truncation - lower], axis=2).reshape(n_wave, 2 * pairs)
    waves = jnp.concatenate([held[:, :ROWS].reshape(-1), held[:, ROWS:].T.reshape(-1)]).reshape(1, truncation + 1)
    return place_waves(waves, received, lat_dev)


def solution(mesh):
    placed = (P("wave", None, None, "fld"), P("wave", None, None, "fld"), P(), P(), P())
    return jax.shard_map(
        on_device, mesh=mesh, in_specs=placed, out_specs=P("wave", None, "fld"), check_vma=False
    )
```

```python
import functools

import jax
import jax.numpy as jnp
from jax import lax
from jax.experimental import pallas as pl
from jax.experimental.pallas import tpu as pltpu
from jax.sharding import PartitionSpec as P

BF = jnp.bfloat16
F32 = jnp.float32
LANES = 128
ROWS = 16
PLAIN = 2
VMEM = pl.BlockSpec(memory_space=pltpu.VMEM)
SMEM = pl.BlockSpec(memory_space=pltpu.SMEM)
LEFT = 4
PARAMS = pltpu.CompilerParams(vmem_limit_bytes=24 * 1024 * 1024)


def pack_kernel(first, table_ref, out_ref, held_ref, sem):
    group, _, rows, half_slots = held_ref.shape
    blocks = half_slots // LANES
    fetch = pltpu.make_async_copy(table_ref.at[pl.ds(first, group)], held_ref, sem)
    fetch.start()
    fetch.wait()
    lane = lax.broadcasted_iota(jnp.int32, (rows, LANES), 1)
    last = jnp.zeros((rows, LANES), F32)
    for i in range(group):
        for r in range(2):
            for b in range(blocks):
                out_ref[(2 * i + r) * blocks + b] = held_ref[i, r, :, b * LANES:(b + 1) * LANES]
            tail = held_ref[i, r, :, half_slots - 1:half_slots].astype(F32)
            last = jnp.where(lane == 2 * i + r, tail, last)
    out_ref[2 * group * blocks] = last.astype(BF)


def pack_table(table, groups):
    pairs, _, rows, half_slots = table.shape
    assert half_slots % LANES == 1
    group = pairs // groups
    length = 2 * group * (half_slots // LANES) + 1
    return [
        pl.pallas_call(
            functools.partial(pack_kernel, g * group),
            in_specs=[pl.BlockSpec(memory_space=pltpu.HBM)],
            out_specs=VMEM,
            out_shape=jax.ShapeDtypeStruct((length, rows, LANES), BF),
            scratch_shapes=[pltpu.VMEM((group, 2, rows, half_slots), BF), pltpu.SemaphoreType.DMA],
            compiler_params=PARAMS,
            name="pack_table",
        )(table)
        for g in range(groups)
    ]


def even_partner(z):
    return z + 1 - 2 * (z % 2)


def odd_partner(z, n):
    return (z + n - 1 + 2 * (z % 2)) % n


def held_order(z, n, first):
    partners = [even_partner, lambda i: odd_partner(i, n)]
    near, far = partners[first], partners[1 - first]
    pairs, via = [(z, near(z))], z
    for step in range(1, n // 2):
        origin, path = z, []
        for k in range(step):
            path.append(far if (step - k) % 2 else near)
        for move in path:
            origin = move(origin)
        pairs.append((origin, near(origin)))
    return [i for pair in pairs for i in pair]


def rows_kernel(lat_dev, place_ref, slots_ref, points_ref, *out_refs):
    pick_refs, limit_ref = out_refs[:-1], out_refs[-1]
    lats = slots_ref.shape[1]
    half = lats // 2
    n_wave = lats // lat_dev
    sent = lax.broadcasted_iota(jnp.int32, (lats, lats), 1)
    source = lax.rem(sent, n_wave) * lat_dev + sent // n_wave
    moved = jnp.where(lax.broadcasted_iota(jnp.int32, (lats, lats), 0) == source, 1.0, 0.0).astype(BF)
    slots = jnp.broadcast_to(slots_ref[...].astype(F32), (ROWS, lats)).astype(BF)
    slots = jnp.dot(slots, moved, preferred_element_type=F32)[:1].astype(jnp.int32)
    cycle = lax.rem(slots, half)
    index = lax.broadcasted_iota(jnp.int32, (lats, lats), 0)
    for first, pick_ref in enumerate(pick_refs):
        held = lax.rem(cycle, ROWS) + (slots // half) * half
        for at, z in enumerate(held_order(place_ref[1], half // ROWS, first)):
            held = held + jnp.where(cycle // ROWS == z, at * ROWS, 0)
        pick_ref[...] = jnp.where(index == held, 1.0, 0.0).T.astype(BF)
    index = lax.broadcasted_iota(jnp.int32, (half, lats), 0)
    points = jnp.where(index == cycle, 1.0, 0.0).T * points_ref[...].astype(F32)
    limit_ref[...] = jnp.broadcast_to(jnp.sum(points, axis=1, keepdims=True), limit_ref.shape)


def row_order(place, slots, points, lat_dev):
    lats = slots.shape[1]
    assert lats <= 256
    return pl.pallas_call(
        functools.partial(rows_kernel, lat_dev),
        in_specs=[SMEM, VMEM, VMEM],
        out_specs=[VMEM] * 3,
        out_shape=[jax.ShapeDtypeStruct((lats, lats), BF)] * 2 + [jax.ShapeDtypeStruct((lats, LANES), F32)],
        compiler_params=PARAMS,
        name="row_order",
    )(place, slots, points)


def sent_row(pair, h, lat, lat_dev):
    row = 2 * pair + h
    return lat * ROWS + row if row < ROWS else lat_dev * ROWS + lat * LEFT + row - ROWS


def sums_kernel(truncation, n_wave, first_pair, last_group, place_ref, lower_ref, pick_ref, limit_ref, spec_ref, *refs):
    shard_refs, earlier, out_ref = refs[:5], refs[5:-2] if last_group else (), refs[-2] if last_group else refs[-1]
    rows_ref = refs[-1]
    all_pairs, _, half_slots, columns = spec_ref.shape
    lat_dev = pick_ref.shape[0] // n_wave
    per_dev = rows_ref.shape[0] // n_wave
    group = all_pairs // 2
    full = half_slots - 1
    blocks = full // LANES
    plain = PLAIN * LANES

    def block(b):
        length = shard_refs[0].shape[0]
        parts = [ref[b + at] for ref in shard_refs for at in range(0, ref.shape[0], length)]
        return jnp.concatenate(parts, axis=0)

    def step(i):
        for pair in (i + first_pair,):
            q = lower_ref[place_ref[0] * all_pairs + pair]
            length = truncation + 1 - q
            begin = length + lax.rem(length, 2)
            tails = block(2 * group * blocks)
            sums = []
            for r in range(2):
                def owned(slot, coeffs, lower):
                    kept = slot < length if lower else (slot >= begin) & (slot <= begin + q)
                    return jnp.where(kept, coeffs, 0.0).astype(BF)

                table = [block((2 * i + r) * blocks + b) for b in range(blocks)]
                below = jnp.dot(
                    jnp.concatenate(table[:PLAIN], axis=1), spec_ref[pair, r, :plain, :], preferred_element_type=F32
                )
                coeffs = spec_ref[pair, r, plain:full, :].astype(F32)
                slot = 2 * (lax.broadcasted_iota(jnp.int32, coeffs.shape, 0) + plain) + r
                row = lax.broadcasted_iota(jnp.int32, (LANES, columns), 0)
                tail = jnp.where(row == 2 * i + r, spec_ref[pair, r, full:, :].astype(F32), 0.0)
                last = jnp.full((LANES, columns), 2 * full + r, jnp.int32)
                both = [
                    jnp.concatenate([owned(slot, coeffs, lower), owned(last, tail, lower)], axis=0)
                    for lower in (True, False)
                ]
                above = jnp.dot(
                    jnp.concatenate(table[PLAIN:] + [tails], axis=1),
                    jnp.concatenate(both, axis=1),
                    preferred_element_type=F32,
                )
                sums.append((above[:, :columns] + below, above[:, columns:]))
            north = jnp.concatenate([sums[0][h] + sums[1][h] for h in range(2)], axis=1)
            south = jnp.concatenate([sums[0][h] - sums[1][h] for h in range(2)], axis=1)
            fourier = jnp.concatenate([north, south], axis=0).astype(BF)
            picked = jnp.dot(pick_ref[...], fourier, preferred_element_type=F32)
            for h in range(2):
                wave = (q if h == 0 else truncation - q).astype(F32)
                kept = jnp.where(2.0 * wave < limit_ref[...], picked[:, h * columns:(h + 1) * columns], 0.0)
                for lat in range(lat_dev):
                    at = pl.ds(sent_row(pair, h, lat, lat_dev), n_wave, stride=per_dev)
                    rows_ref[at, :] = kept[lat * n_wave:(lat + 1) * n_wave]

    for i in range(group):
        step(i)

    def narrow(d, carry):
        base = pl.multiple_of(d * per_dev, per_dev)
        parts = []
        for at in range(0, per_dev, 8):
            there = 2 * group - at % ROWS if at < lat_dev * ROWS else 0
            rows = pl.ds(base + at, 8)
            if there <= 0:
                parts.append(rows_ref[rows, :])
            elif there >= 8:
                parts.append(earlier[0][rows, :])
            else:
                row = lax.broadcasted_iota(jnp.int32, (8, columns), 0)
                parts.append(jnp.where(row < there, earlier[0][rows, :], rows_ref[rows, :]))
        out_ref[pl.ds(base, per_dev), :] = jnp.concatenate(parts, axis=0).astype(BF)
        return carry

    if last_group:
        lax.fori_loop(0, n_wave, narrow, 0, unroll=16)


def legendre_sums(place, pair_lower, pick, limit, spec, shards, earlier, first_pair, group, last, n_wave, truncation):
    columns = spec.shape[3]
    rows = 4 * group * pick.shape[0]
    out = jax.ShapeDtypeStruct((rows, columns), BF if last else F32)
    return pl.pallas_call(
        functools.partial(sums_kernel, truncation, n_wave, first_pair, last),
        in_specs=[SMEM, SMEM] + [VMEM] * (3 + len(shards) + len(earlier)),
        out_specs=VMEM,
        out_shape=out,
        scratch_shapes=[pltpu.VMEM((rows, columns), F32)] if last else [],
        compiler_params=PARAMS,
        name="legendre_sums",
    )(place, pair_lower, pick, limit, spec, *shards, *earlier)


def place_kernel(waves_ref, received_ref, out_ref, rows_ref, left_ref, placed_ref, sems):
    lat_dev, count, columns = placed_ref.shape
    n_wave = received_ref.shape[0]
    main = n_wave * ROWS
    rows_ref[...] = received_ref[:, lat_dev * ROWS:, :].astype(F32).reshape(rows_ref.shape)
    for lat in range(lat_dev):
        for i in range(LEFT):
            rows = rows_ref[pl.ds(lat * LEFT + i, n_wave, stride=lat_dev * LEFT), :]
            left_ref[i * n_wave:(i + 1) * n_wave, lat * columns:(lat + 1) * columns] = rows.astype(BF)
    held = [received_ref[:, lat * ROWS:(lat + 1) * ROWS, :].reshape(main, columns) for lat in range(lat_dev)]
    held = jnp.concatenate([jnp.concatenate(held, axis=1), left_ref[...]], axis=0)
    tall = count // 4
    copies = []
    for n in range(4):
        index = lax.broadcasted_iota(jnp.int32, (tall, count), 0) + n * tall
        chosen = jnp.where(index == waves_ref[...], 1.0, 0.0).astype(BF)
        placed = jnp.dot(chosen, held, preferred_element_type=F32).astype(BF)
        at = pl.ds(n * tall, tall)
        for lat in range(lat_dev):
            placed_ref[lat, n * tall:(n + 1) * tall, :] = placed[:, lat * columns:(lat + 1) * columns]
        copies.append(pltpu.make_async_copy(placed_ref.at[:, at, :], out_ref.at[:, at, :], sems.at[n]))
        copies[-1].start()
    for copy in copies:
        copy.wait()


def place_waves(waves, received, lat_dev):
    count = waves.shape[1]
    n_wave, _, columns = received.shape
    return pl.pallas_call(
        place_kernel,
        out_specs=pl.BlockSpec(memory_space=pltpu.HBM),
        out_shape=jax.ShapeDtypeStruct((lat_dev, count, columns), BF),
        scratch_shapes=[
            pltpu.VMEM((n_wave * lat_dev * LEFT, columns), F32),
            pltpu.VMEM((n_wave * LEFT, lat_dev * columns), BF),
            pltpu.VMEM((lat_dev, count, columns), BF),
            pltpu.SemaphoreType.DMA((4,)),
        ],
        compiler_params=PARAMS,
        name="place_waves",
    )(waves, received)


def gather_table(groups):
    n = lax.axis_size("fld")
    kinds = [
        [(i, even_partner(i)) for i in range(n)],
        [(i, odd_partner(i, n)) for i in range(n)],
    ]
    held = [[x] for x in groups]
    for step in range(n // 2):
        for first, parts in enumerate(held):
            sent = jnp.concatenate(parts, axis=0) if step == 1 else parts[-1]
            parts.append(lax.ppermute(sent, "fld", kinds[(first + step) % 2]))
    return held


def on_device(spec_coeffs, legendre, pair_lower, slot_latitude, cycle_points):
    pairs, _, half_slots, columns = spec_coeffs.shape
    truncation = 2 * half_slots - 3
    n_wave = lax.axis_size("wave")
    lats = slot_latitude.shape[0]
    lat_dev = lats // n_wave
    group = pairs // 2
    place = jnp.stack([lax.axis_index("wave"), lax.axis_index("fld")]).astype(jnp.int32)
    shards = gather_table(pack_table(jnp.transpose(legendre, (0, 1, 3, 2)), 2))
    *picks, limit = row_order(place, slot_latitude.reshape(1, lats), cycle_points.reshape(1, lats // 2), lat_dev)
    assert 2 * pairs == ROWS + LEFT and lat_dev * LEFT == ROWS
    rows = []
    for g in range(2):
        sums = legendre_sums(
            place, pair_lower, picks[g], limit, spec_coeffs, shards[g], rows, g * group, group, g == 1, n_wave, truncation
        )
        rows.append(sums)
    sent, lower = lax.optimization_barrier((rows[-1].reshape(n_wave, -1, columns), pair_lower))
    received = lax.all_to_all(sent, "wave", split_axis=0, concat_axis=0, tiled=True)
    lower = lower.reshape(n_wave, pairs)
    held = jnp.stack([lower, truncation - lower], axis=2).reshape(n_wave, 2 * pairs)
    waves = jnp.concatenate([held[:, :ROWS].reshape(-1), held[:, ROWS:].T.reshape(-1)]).reshape(1, truncation + 1)
    return place_waves(waves, received, lat_dev)


def solution(mesh):
    placed = (P("wave", None, None, "fld"), P("wave", None, None, "fld"), P(), P(), P())
    return jax.shard_map(
        on_device, mesh=mesh, in_specs=placed, out_specs=P("wave", None, "fld"), check_vma=False
    )
```
